32 devices in a mesh: fsdp: 4 (over z), ctx: 8 (over y, x, core).
Axes of the slice: x: 2, y: 2, z: 4, core: 2. Of those that a mesh axis runs over, the one named last changes fastest.
Arguments:
- hidden: bfloat16 [4, 1024, 8192], P('fsdp', 'ctx'), may hold values from -6 to 6
- values: bfloat16 [4, 1024, 4096], P('fsdp', 'ctx'), may hold values from -6 to 6
- targets: bfloat16 [4, 1024, 4096], P('fsdp', 'ctx'), may hold values from -6 to 6
- dt_raw: float32 [4, 32, 1024], P('fsdp', None, 'ctx'), as said below
- proj_weight: bfloat16 [8192, 128], P('fsdp'), may hold values from -0.0234375 to 0.0234375
- a_log: float32 [32], replicated
- skip: float32 [32], replicated, may hold values from 0.5 to 1.5
Outputs:
- grad_w: float32 [8192, 128], P('fsdp')
- grad_a_log: float32 [32], replicated
- grad_skip: float32 [32], replicated
- loss: float32 [], replicated
The draws below stay inside these ranges and needn't reach their ends.
Inputs may be any that keep to these rules, and one draw needn't show every extreme that they name: softplus(dt_raw) is the step size of a head at a position.
All inputs are finite; a program needn't handle non-finite values.
Results may differ from the reference program's by a relative error of at most 0.004.
Values may be sent and summed in bfloat16 or wider, within the bound.
No kernel may reach another device: no remote copies, remote signals or barrier semaphores. Data moves between devices by JAX's collectives and lax.ppermute only.
A program may use at most 192 MiB of HBM per device.

```python
import math
import jax
import jax.numpy as jnp
from jax import lax

D = 8192
HEADS = 32
HDIM = 128
STATE = 64
TOK_DEV = 128
SEQS = 4
LEN = 1024
INNER = 4096


def draw_dt_raw(key, part):
    first, second = jax.random.split(jax.random.fold_in(key, 11))
    blocks = LEN // TOK_DEV
    device_scale = jnp.exp(jax.random.uniform(first, (SEQS, 1, blocks, 1), jnp.float32, -0.7, 0.7))
    cell_scale = jnp.exp(jax.random.uniform(second, (SEQS, HEADS, blocks, TOK_DEV), jnp.float32, -0.7, 0.7))
    step_size = 1.5 / math.sqrt(LEN) * device_scale * cell_scale
    step_size = step_size.reshape(SEQS, HEADS, LEN)
    return jnp.log(jnp.expm1(step_size))


def draw_a_log(key, part):
    spot = jax.random.uniform(jax.random.fold_in(key, 23), (HEADS,), jnp.float32)
    spot = spot ** 3
    per_step = jnp.exp(spot * math.log(max(LEN / 30.0, 4.0))) / LEN
    rate = per_step * math.sqrt(LEN) / 1.5
    return jnp.log(rate)


def raised(entries, key, source, target, parts, factor):
    def block_of(axis_at):
        return (jnp.arange(entries.shape[axis_at]) // (entries.shape[axis_at] // parts)).reshape((-1,) + (1,) * (entries.ndim - 1 - axis_at))

    first = jax.random.permutation(key, parts)[block_of(target)]
    second = (block_of(target) + parts // 2) % parts
    return jnp.where((block_of(source) == first) | (block_of(source) == second), factor * entries, entries)


def levels(rng, extent, cuts, least, high):
    loudness, own = 1.0, jax.random.fold_in(rng, 6)
    for dim, parts in cuts:
        heights = jnp.exp(jax.random.uniform(jax.random.fold_in(own, dim), (parts,), jnp.float32, least / len(cuts), high / len(cuts)))
        loudness = loudness * jnp.repeat(heights, extent[dim] // parts).reshape([-1 if axis == dim else 1 for axis in range(len(extent))])
    return loudness


def bell_draw(own_key, extent, deviation, reach, shards=(), held_as=jnp.bfloat16):
    level = levels(own_key, extent, shards, -0.22, 0.18) if shards else 1.0
    drawn = jax.random.normal(own_key, extent, jnp.float32) * deviation * level
    return jnp.minimum(jnp.maximum(drawn, -reach), reach).astype(held_as)


def heavy_noise(key, extent, deviation, limit, shards, heavy, kind=jnp.bfloat16):
    drawn = deviation * jax.random.normal(key, extent, jnp.float32)
    if shards:
        drawn = drawn * levels(key, extent, shards, -0.22, 0.18)
    return jnp.clip(raised(drawn, jax.random.fold_in(key, 3), *heavy), -limit, limit).astype(kind)


def setup_inputs(seed: int = 0) -> dict:
    splits = jax.random.split(jax.random.key(seed), 8)
    hidden = heavy_noise(splits[0], (SEQS, LEN, D), 1.0, 6.0, ((0, 4), (1, 8)), (0, 2, 4, 2.0))
    values = bell_draw(splits[1], (SEQS, LEN, INNER), 1.0, 6.0, ((0, 4), (1, 8)))
    targets = bell_draw(splits[2], (SEQS, LEN, INNER), 1.0, 6.0, ((0, 4), (1, 8)))
    dt_raw = draw_dt_raw(jax.random.fold_in(splits[7], 71), 0)
    proj_weight = bell_draw(splits[4], (D, 2 * STATE), (8 * D) ** -0.5, 0.0234375, ((0, 4),))
    a_log = draw_a_log(jax.random.fold_in(splits[7], 71), 0)
    skip = jnp.clip(jax.random.uniform(splits[6], (HEADS,), jnp.float32, 0.5, 1.5), 0.5, 1.5)
    return dict(hidden=hidden, values=values, targets=targets, dt_raw=dt_raw, proj_weight=proj_weight, a_log=a_log, skip=skip)


highest = lax.Precision.HIGHEST

def product(form, left, right):
    left, right = lax.optimization_barrier((left, right))
    return jnp.einsum(form, left.astype(jnp.float32), right.astype(jnp.float32), precision=highest)

def block_local(proj, step_size, decay_rate, vals, lower_mask):
    row_count = proj.shape[0]
    head_count = step_size.shape[0]
    state_width = proj.shape[1] // 2
    input_map = proj[:, :state_width]
    output_map = proj[:, state_width:]
    decay_sum = jnp.cumsum(step_size * decay_rate[:, None], axis=1)
    final = decay_sum[:, -1:]
    scores = jnp.dot(output_map, input_map.T, preferred_element_type=jnp.float32)
    within = jnp.where(lower_mask[None] > 0, jnp.exp(jnp.minimum(decay_sum[:, :, None] - decay_sum[:, None, :], 0.0)), 0.0)
    mixing = within * scores[None] * step_size[:, None, :]
    inputs = vals.reshape(row_count, head_count, vals.shape[1] // head_count)
    inner_out = product('hts,shp->thp', mixing.astype(jnp.bfloat16), inputs)
    to_end = jnp.exp(final - decay_sum)
    weight_end = to_end * step_size
    coef = (weight_end[:, None, :] * input_map.T.astype(jnp.float32)[None]).astype(jnp.bfloat16)
    local_state = product('hns,shp->hnp', coef, inputs)
    growth = jnp.exp(decay_sum)
    carry = jnp.exp(final[:, 0])
    return (input_map, output_map, step_size, decay_sum, within, mixing, inputs, to_end, weight_end, growth, local_state, carry, inner_out)

def block_output(pack, state_in, wanted, skip_gain):
    input_map, output_map, step_size, decay_sum, within, mixing, inputs, to_end, weight_end, growth, local_state, carry, inner_out = pack
    state_bf = state_in.astype(jnp.bfloat16)
    from_state = product('hnp,tn->thp', state_bf, output_map)
    outputs = inner_out + growth.T[:, :, None] * from_state + skip_gain[None, :, None] * inputs.astype(jnp.float32)
    misfit = outputs - wanted.reshape(inputs.shape).astype(jnp.float32)
    return (misfit, from_state, state_bf)

def block_return(pack, from_state, state_bf, misfit, loss_scale):
    input_map, output_map, step_size, decay_sum, within, mixing, inputs, to_end, weight_end, growth, local_state, carry, inner_out = pack
    grad_out = misfit * loss_scale
    skip_part = lax.optimization_barrier(jnp.sum(grad_out * inputs.astype(jnp.float32), axis=(0, 2)))
    grad_bf = grad_out.astype(jnp.bfloat16)
    mix_grad = product('thp,shp->hts', grad_bf, inputs)
    score_grad = lax.optimization_barrier(jnp.sum(within * mix_grad * step_size[:, None, :], axis=0))
    weighted = mix_grad * mixing
    sum_grad = lax.optimization_barrier(jnp.sum(weighted, axis=2)) - lax.optimization_barrier(jnp.sum(weighted, axis=1)) + growth * lax.optimization_barrier(jnp.sum(grad_out * from_state, axis=2)).T
    grown_bf = (growth.T[:, :, None] * grad_out).astype(jnp.bfloat16)
    entry_grad = product('thp,tn->hnp', grown_bf, output_map)
    score_bf = score_grad.astype(jnp.bfloat16)
    out_grad = product('thp,hnp->tn', grown_bf, state_bf) + product('ts,sn->tn', score_bf, input_map)
    in_grad = product('ts,tn->sn', score_bf, output_map)
    return (entry_grad, (out_grad, in_grad, sum_grad, skip_part))

def block_finish(pack, partial_value, exit_grad, state_in, decay_rate):
    input_map, output_map, step_size, decay_sum, within, mixing, inputs, to_end, weight_end, growth, local_state, carry, inner_out = pack
    out_grad, in_grad, sum_grad, skip_part = partial_value
    exit_bf = exit_grad.astype(jnp.bfloat16)
    coef_grad = product('hnp,shp->hns', exit_bf, inputs)
    in_grad = in_grad + jnp.einsum('hns,hs->sn', coef_grad, weight_end, precision=highest)
    pulled = jnp.einsum('hns,sn->hs', coef_grad, input_map.astype(jnp.float32), precision=highest)
    end_weight = pulled * weight_end
    final_grad = lax.optimization_barrier(jnp.sum(end_weight, axis=1)) + carry * lax.optimization_barrier(jnp.sum(exit_grad * state_in, axis=(1, 2)))
    row_count = step_size.shape[1]
    last_mark = (jnp.arange(row_count) == row_count - 1).astype(jnp.float32)
    sum_grad = sum_grad - end_weight + final_grad[:, None] * last_mark[None, :]
    step_grad = jnp.cumsum(sum_grad[:, ::-1], axis=1)[:, ::-1]
    alog_part = decay_rate * lax.optimization_barrier(jnp.sum(step_grad * step_size, axis=1))
    proj_grad = jnp.concatenate([in_grad, out_grad], axis=1).astype(jnp.bfloat16)
    return (proj_grad, alog_part, skip_part)

def reference(hidden, values, targets, dt_raw, proj_weight, a_log, skip):
    flat_rows = hidden.reshape(SEQS * LEN, D)
    projection = jnp.dot(flat_rows, proj_weight, preferred_element_type=jnp.float32).astype(jnp.bfloat16)
    projection = projection.reshape(SEQS, LEN, 2 * STATE)
    decay_rate = -jnp.exp(a_log)
    loss_scale = 1.0 / (INNER * math.sqrt(SEQS * LEN))
    blocks = LEN // TOK_DEV
    position = jnp.arange(TOK_DEV)
    lower_mask = (position[:, None] >= position[None, :]).astype(jnp.float32)

    def one_sequence(totals, seq_items):
        proj_s, raw_s, vals_s, goal_s = seq_items
        step_all = jax.nn.softplus(raw_s)
        proj_b = proj_s.reshape(blocks, TOK_DEV, 2 * STATE)
        step_b = step_all.reshape(HEADS, blocks, TOK_DEV).transpose(1, 0, 2)
        vals_b = vals_s.reshape(blocks, TOK_DEV, INNER)
        goal_b = goal_s.reshape(blocks, TOK_DEV, INNER)

        def advance(state_in, block_items):
            proj_k, step_k, vals_k, goal_k = block_items
            local_pack = block_local(proj_k, step_k, decay_rate, vals_k, lower_mask)
            misfit, from_state, state_bf = block_output(local_pack, state_in, goal_k, skip)
            entry_grad, partial_value = block_return(local_pack, from_state, state_bf, misfit, loss_scale)
            new_state = local_pack[11][:, None, None] * state_in + local_pack[10]
            return (new_state, (state_in, local_pack[11], entry_grad, jnp.sum(misfit * misfit)))
        zero_state = jnp.zeros((HEADS, STATE, HDIM), jnp.float32)
        ignored, (state_ins, carries, entry_grads, squares) = lax.scan(advance, zero_state, (proj_b, step_b, vals_b, goal_b))

        def retreat(exit_now, block_items):
            carry_k, entry_k = block_items
            return (entry_k + carry_k[:, None, None] * exit_now, exit_now)
        unused, exit_grads = lax.scan(retreat, zero_state, (carries, entry_grads), reverse=True)

        def finish(block_items):
            proj_k, step_k, vals_k, goal_k, state_k, exit_k = block_items
            local_pack = block_local(proj_k, step_k, decay_rate, vals_k, lower_mask)
            misfit, from_state, state_bf = block_output(local_pack, state_k, goal_k, skip)
            entry_grad, partial_value = block_return(local_pack, from_state, state_bf, misfit, loss_scale)
            return block_finish(local_pack, partial_value, exit_k, state_k, decay_rate)
        proj_grads, alog_parts, skip_parts = lax.map(finish, (proj_b, step_b, vals_b, goal_b, state_ins, exit_grads))
        loss_value = 0.5 * loss_scale * jnp.sum(squares)
        updated = (totals[0] + loss_value, totals[1] + lax.optimization_barrier(jnp.sum(alog_parts, axis=0)), totals[2] + lax.optimization_barrier(jnp.sum(skip_parts, axis=0)))
        return (updated, proj_grads.reshape(LEN, 2 * STATE))
    begin = (jnp.zeros((), jnp.float32), jnp.zeros((HEADS,), jnp.float32), jnp.zeros((HEADS,), jnp.float32))
    totals, all_grads = lax.scan(one_sequence, begin, (projection, dt_raw, values, targets))
    grad_w = lax.dot_general(flat_rows, all_grads.reshape(SEQS * LEN, 2 * STATE), (((0,), (0,)), ((), ())), preferred_element_type=jnp.float32)
    return (grad_w, totals[1], totals[2], totals[0])
```

```python
import functools
import math

import jax
import jax.numpy as jnp
from jax import lax
from jax.experimental import pallas as pl
from jax.experimental.pallas import tpu as pltpu
from jax.sharding import PartitionSpec as P

BLOCK = 128
HDIM = 128
PAD = 16


def dot(left, right, dims):
    return lax.dot_general(left, right, (dims, ((), ())), preferred_element_type=jnp.float32)


def fold(value):
    return jnp.sum(value.reshape(value.shape[0] // 8, 8, value.shape[1]), axis=0)


def pieces(value):
    high = value.astype(jnp.bfloat16)
    rest = value - high.astype(jnp.float32)
    middle = rest.astype(jnp.bfloat16)
    return high, middle, (rest - middle.astype(jnp.float32)).astype(jnp.bfloat16)


def running_sum(value):
    lane = lax.broadcasted_iota(jnp.int32, value.shape, 1)
    shift = 1
    while shift < value.shape[1]:
        value += jnp.where(lane >= shift, pltpu.roll(value, shift, 1), 0.0)
        shift *= 2
    return value


def softplus(value):
    small = jnp.exp(-jnp.abs(value))
    series = small * (1.0 - small * (0.5 - small * (1 / 3 - small * (0.25 - small * 0.2))))
    return jnp.maximum(value, 0.0) + jnp.where(small < 0.03, series, jnp.log1p(small))


def prepare_kernel(
    heads, vt_ref, rate_ref, skip_ref, v_ref, within_ref, sloped_ref, base_ref, weighed_ref,
    cols_ref, carry_ref, last_ref, rows_ref,
):
    blocks, tail_at, width = vt_ref.shape[0], vt_ref.shape[1] - PAD, vt_ref.shape[2]
    t_at = lax.broadcasted_iota(jnp.int32, (BLOCK, BLOCK), 0)
    s_at = lax.broadcasted_iota(jnp.int32, (BLOCK, BLOCK), 1)
    mask = t_at >= s_at
    sent = []
    for k in range(blocks):
        rows = vt_ref[k, tail_at:, :].astype(jnp.float32)
        sent.append(rows[:heads] + rows[heads : 2 * heads] + rows[2 * heads : 3 * heads])
    step = softplus(jnp.concatenate(sent, axis=0))
    decay = running_sum(step * rate_ref[...])
    decay_c, step_c = decay.T, step.T
    tail_c = decay_c[BLOCK - 1 :, :] - decay_c
    growth_c = jnp.exp(decay_c)
    end_c = jnp.exp(tail_c) * step_c
    rise_c = growth_c * decay_c

    def spread(row):
        each = [jnp.broadcast_to(row[:, h : h + 1], (1, width)) for h in range(heads)]
        return jnp.concatenate(each, axis=1)

    for k in range(blocks):
        own = slice(k * heads, (k + 1) * heads)
        made = (growth_c, rise_c, end_c, tail_c, decay_c)
        cols_ref[k] = jnp.concatenate([x[:, own] for x in made], axis=1)
        rows_ref[k, :heads, :] = decay[own, :]
        rows_ref[k, heads:, :] = step[own, :]
        carry_ref[k] = spread(growth_c[BLOCK - 1 :, own])
        last_ref[k] = spread(rise_c[BLOCK - 1 :, own])

    def block(k, carry):
        cols, rows = cols_ref[k], rows_ref[k]
        for h in range(heads):
            i = k * heads + h
            col = lambda j: cols[:, j * heads + h : j * heads + h + 1]
            diff = jnp.minimum(col(4) - rows[h : h + 1, :], 0.0)
            within = jnp.where(mask, jnp.exp(diff), 0.0) * rows[heads + h : heads + h + 1, :]
            within_ref[i] = within
            sloped_ref[i] = within * diff
            v = vt_ref[k, h * BLOCK : (h + 1) * BLOCK, :]
            goal = vt_ref[k, (heads + h) * BLOCK : (heads + h + 1) * BLOCK, :]
            vf = v.astype(jnp.float32)
            v_ref[i] = v
            base_ref[i] = skip_ref[h] * vf - goal.astype(jnp.float32)
            weighed_ref[k, :, h * width : (h + 1) * width] = (vf * col(2)).astype(jnp.bfloat16)
        return carry

    lax.fori_loop(0, blocks, block, 0)


def mixer_kernel(
    heads, scale, count, maps_ref, v_ref, within_ref, sloped_ref, base_ref, weighed_ref, cols_ref,
    carry_ref, last_ref, first_ref, out_ref, pack_ref, states, entries, parts, stat_ref,
):
    blocks, width = cols_ref.shape[0], v_ref.shape[2]
    half = maps_ref.shape[1] // 2
    full = heads * width
    stat_ref[...] = jnp.zeros_like(stat_ref)

    def forward(k, state):
        at = pl.ds(pl.multiple_of(k * BLOCK, BLOCK), BLOCK)
        maps, cols = maps_ref[at, :], cols_ref[k]
        b, c = maps[:, :half], maps[:, half:]
        scores = dot(c, b, ((1,), (1,)))
        state_bf = state.astype(jnp.bfloat16)
        states[k] = state
        from_all = dot(c, state_bf, ((1,), (0,)))
        score_grad = jnp.zeros((BLOCK, BLOCK), jnp.float32)
        grown = []
        for h in range(heads):
            i = k * heads + h
            v, within = v_ref[i], within_ref[i]
            growth, rise = cols[:, h : h + 1], cols[:, heads + h : heads + h + 1]
            inner = dot((within * scores).astype(jnp.bfloat16), v, ((1,), (0,)))
            from_state = from_all[:, h * width : (h + 1) * width]
            misfit = inner + growth * from_state + base_ref[i]
            grad = misfit * scale
            mix_grad = dot(grad.astype(jnp.bfloat16), v, ((1,), (1,)))
            grown.append((grad * growth).astype(jnp.bfloat16))
            stat_ref[h, 0] += fold(misfit * misfit)
            stat_ref[h, 1] += fold(grad * v.astype(jnp.float32))
            stat_ref[h, 2] += fold(grad * from_state * rise)
            score_grad += within * mix_grad
            stat_ref[h, 2] += fold(mix_grad * scores * sloped_ref[i])
        grown = jnp.concatenate(grown, axis=1)
        entries[k] = dot(c, grown, ((0,), (0,)))
        score_bf = score_grad.astype(jnp.bfloat16)
        grad_c = dot(grown, state_bf, ((1,), (1,))) + dot(score_bf, b, ((1,), (0,)))
        grad_b = dot(score_bf, c, ((0,), (0,)))
        parts[at, :] = jnp.concatenate([grad_b, grad_c], axis=1)
        return carry_ref[k] * state + dot(b, weighed_ref[k], ((0,), (0,)))

    unrolled(blocks, forward, jnp.zeros((half, full), jnp.float32))

    def backward(i, leaving):
        k = blocks - 1 - i
        at = pl.ds(pl.multiple_of(k * BLOCK, BLOCK), BLOCK)
        bf = maps_ref[at, :][:, :half].astype(jnp.float32)
        cols = cols_ref[k]
        leaving_bf = leaving.astype(jnp.bfloat16)
        grad_b = jnp.zeros((BLOCK, half), jnp.float32)
        overlap = leaving * states[k] * last_ref[k]
        for h in range(heads):
            piece = slice(h * width, (h + 1) * width)
            coef_grad = dot(v_ref[k * heads + h], leaving_bf[:, piece], ((1,), (1,)))
            pulled = coef_grad * cols[:, 2 * heads + h : 2 * heads + h + 1]
            grad_b += pulled
            tail = cols[:, 3 * heads + h : 3 * heads + h + 1]
            stat_ref[h, 2, :, :half] += fold(pulled * bf * tail)
            stat_ref[h, 2] += fold(overlap[:, piece])
        both = jnp.concatenate([grad_b, jnp.zeros_like(grad_b)], axis=1)
        out_ref[at, :] = (parts[at, :] + both).astype(out_ref.dtype)
        return entries[k] + carry_ref[k] * leaving

    unrolled(blocks, backward, jnp.zeros((half, full), jnp.float32))

    lane = lax.broadcasted_iota(jnp.int32, (1, 128), 1)
    packed = jnp.zeros((1, 128), jnp.float32)
    for h in range(heads):
        at_head = first_ref[0] + h
        sums = [jnp.sum(stat_ref[h, i]) for i in range(3)]
        packed += jnp.where(lane == at_head, sums[2], 0.0)
        packed += jnp.where(lane == count + at_head, sums[1], 0.0)
        packed += jnp.where(lane == 2 * count, 0.5 * scale * sums[0], 0.0)
    pack_ref[...] = jnp.zeros_like(pack_ref)
    for i, piece in enumerate(pieces(packed)):
        pack_ref[i : i + 1, :] = piece


def unrolled(count, step, start):
    each = 4 if count % 4 == 0 else 1

    def several(i, value):
        for j in range(each):
            value = step(i * each + j, value)
        return value

    return lax.fori_loop(0, count // each, several, start)


VMEM = pl.BlockSpec(memory_space=pltpu.VMEM)
SMEM = pl.BlockSpec(memory_space=pltpu.SMEM)
ANY = pl.BlockSpec(memory_space=pl.ANY)
LIMIT = 28 * 1024 * 1024


def prepare(vt, rates, skip):
    blocks, rows, width = vt.shape
    heads = (rows - PAD) // BLOCK // 2
    units, full = blocks * heads, heads * width
    square = jax.ShapeDtypeStruct((units, BLOCK, BLOCK), jnp.float32)
    row = jax.ShapeDtypeStruct((blocks, 1, full), jnp.float32)
    return pl.pallas_call(
        functools.partial(prepare_kernel, heads),
        out_shape=(
            jax.ShapeDtypeStruct((units, BLOCK, width), jnp.bfloat16),
            square,
            square,
            jax.ShapeDtypeStruct((units, BLOCK, width), jnp.float32),
            jax.ShapeDtypeStruct((blocks, BLOCK, full), jnp.bfloat16),
            jax.ShapeDtypeStruct((blocks, BLOCK, 5 * heads), jnp.float32),
            row,
            row,
        ),
        in_specs=[VMEM, VMEM, SMEM],
        out_specs=(VMEM,) * 8,
        scratch_shapes=[pltpu.VMEM((blocks, 2 * heads, BLOCK), jnp.float32)],
        compiler_params=pltpu.CompilerParams(vmem_limit_bytes=LIMIT),
        name="prepare",
    )(vt, rates, skip)


def mixer(maps, ready, first, scale, count):
    length, both = maps.shape
    units, _, width = ready[0].shape
    blocks = length // BLOCK
    heads = units // blocks
    full = heads * width
    return pl.pallas_call(
        functools.partial(mixer_kernel, heads, scale, count),
        out_shape=(
            jax.ShapeDtypeStruct((length, both), jnp.bfloat16),
            jax.ShapeDtypeStruct((PAD, 128), jnp.bfloat16),
        ),
        in_specs=[VMEM] * 9 + [SMEM],
        out_specs=(VMEM, VMEM),
        scratch_shapes=[
            pltpu.VMEM((blocks, both // 2, full), jnp.float32),
            pltpu.VMEM((blocks, both // 2, full), jnp.float32),
            pltpu.VMEM((length, both), jnp.float32),
            pltpu.VMEM((heads, 3, 8, 128), jnp.float32),
        ],
        compiler_params=pltpu.CompilerParams(vmem_limit_bytes=LIMIT),
        cost_estimate=pl.CostEstimate(
            flops=14 * length * BLOCK * full, bytes_accessed=6 * length * full, transcendentals=0
        ),
        name="mixer",
    )(maps, *ready, first.reshape(1))


def pack_mixer_kernel(
    core_ref, values_hbm, targets_hbm, dt_ref, weight_hbm, out_hbm, part_ref, held, out_ref,
    weight_sem, in_sems, sems,
):
    count, rows, width = out_ref.shape
    heads = (rows - PAD) // BLOCK // 2
    loads = []
    for c in range(count):
        own = pl.ds(c * heads * width, heads * width)
        for i, ref in enumerate((values_hbm, targets_hbm)):
            copy = pltpu.make_async_copy(ref.at[0, :, own], held.at[c, i], in_sems.at[c, i])
            copy.start()
            loads.append(copy)
    half = part_ref.shape[0]
    at = pl.multiple_of(core_ref[0] * half, half)
    load = pltpu.make_async_copy(weight_hbm.at[pl.ds(at, half), :], part_ref, weight_sem)
    load.start()
    for c in range(count):
        sent = [x.astype(jnp.float32) for x in pieces(dt_ref[0, c * heads : (c + 1) * heads, :])]
        sent.append(jnp.zeros((PAD - 3 * heads, width), jnp.float32))
        out_ref[c, rows - PAD :, :] = jnp.concatenate(sent, axis=0).astype(jnp.bfloat16)
    stores = []
    for c in range(count):
        for i in range(2):
            loads[2 * c + i].wait()
            for h in range(heads):
                to = (i * heads + h) * BLOCK
                out_ref[c, to : to + BLOCK, :] = held[c, i, :, h * width : (h + 1) * width]
        stores.append(pltpu.make_async_copy(out_ref.at[c], out_hbm.at[c], sems.at[c]))
        stores[c].start()
    load.wait()
    for copy in stores:
        copy.wait()


def pack_mixer(core, values, targets, dt_raw, weight, ctx):
    rows, width = values.shape[1:]
    heads = dt_raw.shape[1] // ctx
    shape = (ctx, 2 * heads * BLOCK + PAD, HDIM)
    return pl.pallas_call(
        pack_mixer_kernel,
        out_shape=(
            jax.ShapeDtypeStruct(shape, jnp.bfloat16),
            jax.ShapeDtypeStruct((weight.shape[0] // 2, weight.shape[1]), jnp.bfloat16),
        ),
        in_specs=[SMEM, ANY, ANY, VMEM, ANY],
        out_specs=(ANY, VMEM),
        scratch_shapes=[
            pltpu.VMEM((ctx, 2, rows, width // ctx), jnp.bfloat16),
            pltpu.VMEM(shape, jnp.bfloat16),
            pltpu.SemaphoreType.DMA,
            pltpu.SemaphoreType.DMA((ctx, 2)),
            pltpu.SemaphoreType.DMA((ctx,)),
        ],
        name="pack_mixer",
    )(core.reshape(1), values, targets, dt_raw, weight)


def pack_hidden_kernel(half, core_ref, hidden_ref, out_ref):
    for f in range(out_ref.shape[1] // half):
        at = pl.multiple_of((2 * f + core_ref[0]) * half, half)
        out_ref[:, f * half : (f + 1) * half] = hidden_ref[0, :, pl.ds(at, half)]


def pack_hidden(core, hidden, half):
    _, rows, width = hidden.shape
    return pl.pallas_call(
        functools.partial(pack_hidden_kernel, half),
        out_shape=jax.ShapeDtypeStruct((rows, width // 2), jnp.bfloat16),
        in_specs=[SMEM, VMEM],
        out_specs=VMEM,
        compiler_params=pltpu.CompilerParams(vmem_limit_bytes=LIMIT),
        name="pack_hidden",
    )(core.reshape(1), hidden)


def project_kernel(half, chunk_ref, hidden_ref, start_ref, *refs):
    weights, out_ref = refs[:-1], refs[-1]
    total = start_ref[...]
    j = 0
    for weight_ref in weights:
        for i in range(weight_ref.shape[0] // half):
            at = pl.multiple_of(chunk_ref[j] * half, half)
            block = weight_ref[i * half : (i + 1) * half, :]
            total += dot(hidden_ref[0, :, pl.ds(at, half)], block, ((1,), (0,)))
            j += 1
    out_ref[...] = total.astype(out_ref.dtype)


def project(chunks, hidden, weights, start, kind):
    half = sum(weight.shape[0] for weight in weights) // len(chunks)
    return pl.pallas_call(
        functools.partial(project_kernel, half),
        out_shape=jax.ShapeDtypeStruct(start.shape, kind),
        in_specs=[SMEM] + [VMEM] * (2 + len(weights)),
        out_specs=VMEM,
        compiler_params=pltpu.CompilerParams(vmem_limit_bytes=LIMIT),
        name="project",
    )(jnp.stack(chunks).astype(jnp.int32), hidden, start, *weights)


def put_scalars(out_ref, at, tails):
    parts = pieces(jnp.sum(tails, axis=0, keepdims=True))
    out_ref[at:, :] = jnp.zeros((PAD, out_ref.shape[1]), out_ref.dtype)
    for i, part in enumerate(parts):
        out_ref[at + i : at + i + 1, :] = part


def grad_kernel(half, core_ref, near_ref, far_ref, hidden_ref, feats_ref, out_ref):
    chips = out_ref.shape[0]
    slab = half // chips
    step = max(slab, 128)
    near, far = [
        [ref[i * BLOCK : (i + 1) * BLOCK, :] for i in range(2)] for ref in (near_ref, far_ref)
    ]
    for f in range(feats_ref.shape[1] // half):
        for at in range(0, half, step):
            mine = pl.multiple_of((2 * f + core_ref[0]) * half + at, step)
            near_feats = hidden_ref[0, :, pl.ds(mine, step)]
            far_feats = feats_ref[:, f * half + at : f * half + at + step]
            turned = sum(dot(part, near_feats, ((0,), (0,))) for part in near)
            turned += sum(dot(part, far_feats, ((0,), (0,))) for part in far)
            turned = turned.T.astype(out_ref.dtype)
            for i in range(step // slab):
                rows = turned[i * slab : (i + 1) * slab]
                out_ref[at // slab + i, f * slab : (f + 1) * slab, :] = rows
    tails = [ref[2 * BLOCK :, :].astype(jnp.float32) for ref in (near_ref, far_ref)]
    for q in range(chips):
        put_scalars(out_ref.at[q], out_ref.shape[1] - PAD, tails[0] + tails[1])


def weight_grad(core, near, far, hidden, feats, half, chips):
    fsdp = feats.shape[1] // half
    rows = fsdp * half // chips + PAD
    return pl.pallas_call(
        functools.partial(grad_kernel, half),
        out_shape=jax.ShapeDtypeStruct((chips, rows, near.shape[1]), jnp.bfloat16),
        in_specs=[SMEM] + [VMEM] * 4,
        out_specs=VMEM,
        compiler_params=pltpu.CompilerParams(vmem_limit_bytes=LIMIT),
        name="weight_grad",
    )(core.reshape(1), near, far, hidden, feats)


def add_chips_kernel(grad_ref, out_ref):
    fsdp, slab = out_ref.shape[0], out_ref.shape[1] - PAD
    total = jnp.sum(grad_ref[...].astype(jnp.float32), axis=0)
    for f in range(fsdp):
        out_ref[f, :slab, :] = total[f * slab : (f + 1) * slab].astype(out_ref.dtype)
        put_scalars(out_ref.at[f], slab, total[fsdp * slab :])


def add_chips(grad, fsdp):
    _, rows, width = grad.shape
    return pl.pallas_call(
        add_chips_kernel,
        out_shape=jax.ShapeDtypeStruct((fsdp, (rows - PAD) // fsdp + PAD, width), jnp.bfloat16),
        in_specs=[VMEM],
        out_specs=VMEM,
        compiler_params=pltpu.CompilerParams(vmem_limit_bytes=LIMIT),
        name="add_chips",
    )(grad)


def add_kernel(grad_ref, out_ref, alog_ref, skip_ref, loss_ref):
    count, slab = grad_ref.shape[0], out_ref.shape[0]
    heads = alog_ref.shape[1]
    total = jnp.sum(grad_ref[...].astype(jnp.float32), axis=0)
    out_ref[...] = total[:slab].astype(out_ref.dtype)
    total = jnp.sum(total[slab:], axis=0, keepdims=True)
    alog_ref[...] = total[:, :heads]
    skip_ref[...] = total[:, heads : 2 * heads]
    loss_ref[...] = total[:, 2 * heads : 2 * heads + 1]


def add_blocks(grad, heads):
    _, rows, width = grad.shape
    return pl.pallas_call(
        add_kernel,
        out_shape=(
            jax.ShapeDtypeStruct((rows - PAD, width), jnp.bfloat16),
            jax.ShapeDtypeStruct((1, heads), jnp.float32),
            jax.ShapeDtypeStruct((1, heads), jnp.float32),
            jax.ShapeDtypeStruct((1, 1), jnp.float32),
        ),
        in_specs=[VMEM],
        out_specs=(VMEM,) * 4,
        compiler_params=pltpu.CompilerParams(vmem_limit_bytes=LIMIT),
        name="add_blocks",
    )(grad)


def finish_kernel(grad_ref, out_ref):
    count = grad_ref.shape[0]
    for q in range(count // 2):
        for r in range(2):
            out_ref[r * (count // 2) + q] = grad_ref[2 * q + r].astype(jnp.float32)


def finish(grad):
    return pl.pallas_call(
        finish_kernel,
        out_shape=jax.ShapeDtypeStruct(grad.shape, jnp.float32),
        in_specs=[VMEM],
        out_specs=VMEM,
        compiler_params=pltpu.CompilerParams(vmem_limit_bytes=LIMIT),
        name="finish",
    )(grad)


def exchange(blocks, axis):
    return lax.all_to_all(blocks, axis, 0, 0, tiled=True)


def swap(block, axis, shift):
    return lax.ppermute(block, axis, [(i, i ^ shift) for i in range(lax.axis_size(axis))])


def local(hidden, values, targets, dt_raw, proj_weight, a_log, skip):
    fsdp, ctx = lax.axis_size("fsdp"), lax.axis_size("ctx")
    mine = lax.axis_index("ctx")
    core = mine % 2
    rows = hidden.shape[1]
    length = rows * ctx
    heads_all = a_log.shape[0]
    inner = values.shape[2]
    cols = inner // ctx
    heads = cols // HDIM
    half = proj_weight.shape[0] // 2
    slab = proj_weight.shape[0] // ctx
    both = proj_weight.shape[1]
    first = mine * heads
    scale = 1.0 / (inner * math.sqrt(fsdp * length))

    shard = lax.axis_index("fsdp")
    others = [shard ^ shift for shift in range(1, fsdp)]

    vt, part = pack_mixer(core, values, targets, dt_raw, proj_weight, ctx)
    near = [swap(part, "fsdp", shift) for shift in range(1, fsdp)]
    vt = exchange(vt, "ctx")
    a_mine = lax.dynamic_slice_in_dim(a_log, first, heads, 0)
    s_mine = lax.dynamic_slice_in_dim(skip, first, heads, 0)
    rates = jnp.tile(-jnp.exp(a_mine), ctx)[:, None]
    send = pack_hidden(1 - core, hidden, half)
    start = jnp.zeros((rows, both), jnp.float32)
    start = project([2 * shard, 2 * shard + 1], hidden, [proj_weight], start, jnp.float32)
    near, send, rates, s_mine, start = lax.optimization_barrier(
        (near, send, rates, s_mine, start)
    )
    far = [swap(block, "ctx", 1) for block in near]

    near_at = [2 * other + core for other in others]
    far_at = [2 * other + 1 - core for other in others]
    chunks = [at[i] for i in range(fsdp - 1) for at in (near_at, far_at)]
    blocks = [part[i] for i in range(fsdp - 1) for part in (near, far)]
    projection = project(chunks, hidden, blocks, start, jnp.bfloat16)
    projection, vt = lax.optimization_barrier((projection, vt))
    maps = lax.all_gather(projection, "ctx", axis=0, tiled=True)
    maps, send = lax.optimization_barrier((maps, send))
    feats = swap(send, "ctx", 1)

    ready = prepare(vt, rates, s_mine)
    proj_part, packed = mixer(maps, ready, first, scale, heads_all)

    proj_part = exchange(proj_part.reshape(ctx, rows, both), "ctx").astype(jnp.float32)
    proj_grad = jnp.sum(proj_part, axis=0)
    high = lax.reduce_precision(proj_grad, 8, 7)
    proj_grad = [part.astype(jnp.bfloat16) for part in (high, proj_grad - high)]
    proj_grad = jnp.concatenate(proj_grad + [packed], axis=0)
    proj_far = swap(proj_grad, "ctx", 1)

    grad = weight_grad(core, proj_grad, proj_far, hidden, feats, half, ctx // 2)
    chips = [list(range(r, ctx, 2)) for r in range(2)]
    grad = lax.all_to_all(grad, "ctx", 0, 0, tiled=True, axis_index_groups=chips)
    grad = exchange(add_chips(grad, fsdp), "fsdp")
    grad, grad_a, grad_skip, loss = add_blocks(grad, heads_all)
    grad_w = finish(lax.all_gather(grad, "ctx", axis=0)).reshape(ctx * slab, both)
    return (grad_w, grad_a.reshape(heads_all), grad_skip.reshape(heads_all), loss.reshape(()))


def solution(mesh):
    in_specs = (
        P("fsdp", "ctx", None),
        P("fsdp", "ctx", None),
        P("fsdp", "ctx", None),
        P("fsdp", None, "ctx"),
        P("fsdp", None),
        P(),
        P(),
    )
    out_specs = (P("fsdp", None), P(), P(), P())
    return jax.shard_map(local, mesh=mesh, in_specs=in_specs, out_specs=out_specs, check_vma=False)
```

```python
import functools
import math

import jax
import jax.numpy as jnp
from jax import lax
from jax.experimental import pallas as pl
from jax.experimental.pallas import tpu as pltpu
from jax.sharding import PartitionSpec as P

BLOCK = 128
HDIM = 128
PAD = 16


def dot(left, right, dims):
    return lax.dot_general(left, right, (dims, ((), ())), preferred_element_type=jnp.float32)


def fold(value):
    return jnp.sum(value.reshape(value.shape[0] // 8, 8, value.shape[1]), axis=0)


def pieces(value):
    high = value.astype(jnp.bfloat16)
    rest = value - high.astype(jnp.float32)
    middle = rest.astype(jnp.bfloat16)
    return high, middle, (rest - middle.astype(jnp.float32)).astype(jnp.bfloat16)


def running_sum(value):
    lane = lax.broadcasted_iota(jnp.int32, value.shape, 1)
    shift = 1
    while shift < value.shape[1]:
        value += jnp.where(lane >= shift, pltpu.roll(value, shift, 1), 0.0)
        shift *= 2
    return value


def softplus(value):
    small = jnp.exp(-jnp.abs(value))
    series = small * (1.0 - small * (0.5 - small * (1 / 3 - small * (0.25 - small * 0.2))))
    return jnp.maximum(value, 0.0) + jnp.where(small < 0.03, series, jnp.log1p(small))


def mixer_kernel(
    heads, scale, count, maps_ref, vt_hbm, rate_ref, skip_ref, first_ref, out_ref, pack_ref,
    vt_ref, rows_ref, cols_ref, carry_ref, last_ref, states, entries, parts, stat_ref, sems,
):
    blocks, tail_at, width = vt_ref.shape[0], vt_ref.shape[1] - PAD, vt_ref.shape[2]
    half = maps_ref.shape[1] // 2
    full = heads * width
    tail = pltpu.make_async_copy(
        vt_hbm.at[:, pl.ds(tail_at, PAD)], vt_ref.at[:, pl.ds(tail_at, PAD)], sems.at[blocks]
    )
    tail.start()

    def load(k):
        body = pl.ds(0, tail_at)
        return pltpu.make_async_copy(vt_hbm.at[k, body], vt_ref.at[k, body], sems.at[k])

    for k in range(blocks):
        load(k).start()
    stat_ref[...] = jnp.zeros_like(stat_ref)
    t_at = lax.broadcasted_iota(jnp.int32, (BLOCK, BLOCK), 0)
    s_at = lax.broadcasted_iota(jnp.int32, (BLOCK, BLOCK), 1)
    mask = t_at >= s_at
    tail.wait()
    sent = []
    for k in range(blocks):
        rows = vt_ref[k, tail_at:, :].astype(jnp.float32)
        sent.append(rows[:heads] + rows[heads : 2 * heads] + rows[2 * heads : 3 * heads])
    step = softplus(jnp.concatenate(sent, axis=0))
    decay = running_sum(step * rate_ref[...])
    final = decay[:, BLOCK - 1 :]
    growth = jnp.exp(decay)
    tails = final - decay
    made = (growth, growth * decay, jnp.exp(tails) * step, tails, decay, step)
    carry = jnp.broadcast_to(jnp.exp(final), (blocks * heads, width))
    last = jnp.broadcast_to(jnp.exp(final) * final, (blocks * heads, width))
    for k in range(blocks):
        own = slice(k * heads, (k + 1) * heads)
        rows_ref[k] = jnp.concatenate([x[own, :] for x in made], axis=0)
        for h in range(heads):
            one = slice(k * heads + h, k * heads + h + 1)
            carry_ref[k, :, h * width : (h + 1) * width] = carry[one, :]
            last_ref[k, :, h * width : (h + 1) * width] = last[one, :]

    def forward(k, state):
        load(k).wait()
        at = pl.ds(pl.multiple_of(k * BLOCK, BLOCK), BLOCK)
        maps, rows = maps_ref[at, :], rows_ref[k]
        cols = rows.T
        cols_ref[k] = cols
        b, c = maps[:, :half], maps[:, half:]
        scores = dot(c, b, ((1,), (1,)))
        state_bf = state.astype(jnp.bfloat16)
        states[k] = state
        from_all = dot(c, state_bf, ((1,), (0,)))
        score_grad = jnp.zeros((BLOCK, BLOCK), jnp.float32)
        grown, weighed = [], []
        for h in range(heads):
            col = lambda j: cols[:, j * heads + h : j * heads + h + 1]
            v = vt_ref[k, h * BLOCK : (h + 1) * BLOCK, :]
            goal = vt_ref[k, (heads + h) * BLOCK : (heads + h + 1) * BLOCK, :]
            vf = v.astype(jnp.float32)
            row = lambda j: rows[j * heads + h : j * heads + h + 1, :]
            diff = jnp.minimum(col(4) - row(4), 0.0)
            within = jnp.where(mask, jnp.exp(diff), 0.0) * row(5)
            mixing = within * scores
            inner = dot(mixing.astype(jnp.bfloat16), v, ((1,), (0,)))
            from_state = from_all[:, h * width : (h + 1) * width]
            growth = col(0)
            out = inner + growth * from_state + skip_ref[h] * vf
            misfit = out - goal.astype(jnp.float32)
            grad = misfit * scale
            mix_grad = dot(grad.astype(jnp.bfloat16), v, ((1,), (1,)))
            grown.append((grad * growth).astype(jnp.bfloat16))
            weighed.append((vf * col(2)).astype(jnp.bfloat16))
            stat_ref[h, 0] += fold(misfit * misfit)
            stat_ref[h, 1] += fold(grad * vf)
            stat_ref[h, 2] += fold(grad * from_state * col(1))
            score_grad += within * mix_grad
            stat_ref[h, 2] += fold(mix_grad * mixing * diff)
        grown = jnp.concatenate(grown, axis=1)
        weighed = jnp.concatenate(weighed, axis=1)
        entries[k] = dot(c, grown, ((0,), (0,)))
        score_bf = score_grad.astype(jnp.bfloat16)
        grad_c = dot(grown, state_bf, ((1,), (1,))) + dot(score_bf, b, ((1,), (0,)))
        grad_b = dot(score_bf, c, ((0,), (0,)))
        parts[at, :] = jnp.concatenate([grad_b, grad_c], axis=1)
        return carry_ref[k] * state + dot(b, weighed, ((0,), (0,)))

    unrolled(blocks, forward, jnp.zeros((half, full), jnp.float32))

    def backward(i, leaving):
        k = blocks - 1 - i
        at = pl.ds(pl.multiple_of(k * BLOCK, BLOCK), BLOCK)
        bf = maps_ref[at, :][:, :half].astype(jnp.float32)
        cols = cols_ref[k]
        leaving_bf = leaving.astype(jnp.bfloat16)
        grad_b = jnp.zeros((BLOCK, half), jnp.float32)
        overlap = leaving * states[k] * last_ref[k]
        for h in range(heads):
            piece = slice(h * width, (h + 1) * width)
            v = vt_ref[k, h * BLOCK : (h + 1) * BLOCK, :]
            coef_grad = dot(v, leaving_bf[:, piece], ((1,), (1,)))
            pulled = coef_grad * cols[:, 2 * heads + h : 2 * heads + h + 1]
            grad_b += pulled
            tail_w = cols[:, 3 * heads + h : 3 * heads + h + 1]
            stat_ref[h, 2, :, :half] += fold(pulled * bf * tail_w)
            stat_ref[h, 2] += fold(overlap[:, piece])
        both = jnp.concatenate([grad_b, jnp.zeros_like(grad_b)], axis=1)
        out_ref[at, :] = (parts[at, :] + both).astype(out_ref.dtype)
        return entries[k] + carry_ref[k] * leaving

    unrolled(blocks, backward, jnp.zeros((half, full), jnp.float32))

    lane = lax.broadcasted_iota(jnp.int32, (1, 128), 1)
    packed = jnp.zeros((1, 128), jnp.float32)
    for h in range(heads):
        at_head = first_ref[0] + h
        sums = [jnp.sum(stat_ref[h, i]) for i in range(3)]
        packed += jnp.where(lane == at_head, sums[2], 0.0)
        packed += jnp.where(lane == count + at_head, sums[1], 0.0)
        packed += jnp.where(lane == 2 * count, 0.5 * scale * sums[0], 0.0)
    pack_ref[...] = jnp.zeros_like(pack_ref)
    for i, piece in enumerate(pieces(packed)):
        pack_ref[i : i + 1, :] = piece


def unrolled(count, step, start):
    each = 4 if count % 4 == 0 else 1

    def several(i, value):
        for j in range(each):
            value = step(i * each + j, value)
        return value

    return lax.fori_loop(0, count // each, several, start)


VMEM = pl.BlockSpec(memory_space=pltpu.VMEM)
SMEM = pl.BlockSpec(memory_space=pltpu.SMEM)
ANY = pl.BlockSpec(memory_space=pl.ANY)
LIMIT = 28 * 1024 * 1024


def mixer(maps, vt, rates, skip, first, scale, count):
    blocks, rows, width = vt.shape
    length, both = maps.shape
    heads = (rows - PAD) // BLOCK // 2
    full = heads * width
    return pl.pallas_call(
        functools.partial(mixer_kernel, heads, scale, count),
        out_shape=(
            jax.ShapeDtypeStruct((length, both), jnp.bfloat16),
            jax.ShapeDtypeStruct((PAD, 128), jnp.bfloat16),
        ),
        in_specs=[VMEM, ANY, VMEM, SMEM, SMEM],
        out_specs=(VMEM, VMEM),
        scratch_shapes=[
            pltpu.VMEM((blocks, rows, width), jnp.bfloat16),
            pltpu.VMEM((blocks, 6 * heads, BLOCK), jnp.float32),
            pltpu.VMEM((blocks, BLOCK, 6 * heads), jnp.float32),
            pltpu.VMEM((blocks, 1, full), jnp.float32),
            pltpu.VMEM((blocks, 1, full), jnp.float32),
            pltpu.VMEM((blocks, both // 2, full), jnp.float32),
            pltpu.VMEM((blocks, both // 2, full), jnp.float32),
            pltpu.VMEM((length, both), jnp.float32),
            pltpu.VMEM((heads, 3, 8, 128), jnp.float32),
            pltpu.SemaphoreType.DMA((blocks + 1,)),
        ],
        compiler_params=pltpu.CompilerParams(vmem_limit_bytes=LIMIT),
        cost_estimate=pl.CostEstimate(
            flops=14 * length * BLOCK * full, bytes_accessed=6 * length * full, transcendentals=0
        ),
        name="mixer",
    )(maps, vt, rates, skip, first.reshape(1))


def pack_mixer_kernel(
    core_ref, values_hbm, targets_hbm, dt_ref, weight_hbm, out_hbm, part_ref, held, out_ref,
    weight_sem, in_sems, sems,
):
    count, rows, width = out_ref.shape
    heads = (rows - PAD) // BLOCK // 2
    loads = []
    for c in range(count):
        own = pl.ds(c * heads * width, heads * width)
        for i, ref in enumerate((values_hbm, targets_hbm)):
            copy = pltpu.make_async_copy(ref.at[0, :, own], held.at[c, i], in_sems.at[c, i])
            copy.start()
            loads.append(copy)
    half = part_ref.shape[0]
    at = pl.multiple_of(core_ref[0] * half, half)
    load = pltpu.make_async_copy(weight_hbm.at[pl.ds(at, half), :], part_ref, weight_sem)
    load.start()
    for c in range(count):
        sent = [x.astype(jnp.float32) for x in pieces(dt_ref[0, c * heads : (c + 1) * heads, :])]
        sent.append(jnp.zeros((PAD - 3 * heads, width), jnp.float32))
        out_ref[c, rows - PAD :, :] = jnp.concatenate(sent, axis=0).astype(jnp.bfloat16)
    stores = []
    for c in range(count):
        for i in range(2):
            loads[2 * c + i].wait()
            for h in range(heads):
                to = (i * heads + h) * BLOCK
                out_ref[c, to : to + BLOCK, :] = held[c, i, :, h * width : (h + 1) * width]
        stores.append(pltpu.make_async_copy(out_ref.at[c], out_hbm.at[c], sems.at[c]))
        stores[c].start()
    load.wait()
    for copy in stores:
        copy.wait()


def pack_mixer(core, values, targets, dt_raw, weight, ctx):
    rows, width = values.shape[1:]
    heads = dt_raw.shape[1] // ctx
    shape = (ctx, 2 * heads * BLOCK + PAD, HDIM)
    return pl.pallas_call(
        pack_mixer_kernel,
        out_shape=(
            jax.ShapeDtypeStruct(shape, jnp.bfloat16),
            jax.ShapeDtypeStruct((weight.shape[0] // 2, weight.shape[1]), jnp.bfloat16),
        ),
        in_specs=[SMEM, ANY, ANY, VMEM, ANY],
        out_specs=(ANY, VMEM),
        scratch_shapes=[
            pltpu.VMEM((ctx, 2, rows, width // ctx), jnp.bfloat16),
            pltpu.VMEM(shape, jnp.bfloat16),
            pltpu.SemaphoreType.DMA,
            pltpu.SemaphoreType.DMA((ctx, 2)),
            pltpu.SemaphoreType.DMA((ctx,)),
        ],
        name="pack_mixer",
    )(core.reshape(1), values, targets, dt_raw, weight)


def pack_hidden_kernel(half, core_ref, hidden_ref, out_ref):
    for f in range(out_ref.shape[1] // half):
        at = pl.multiple_of((2 * f + core_ref[0]) * half, half)
        out_ref[:, f * half : (f + 1) * half] = hidden_ref[0, :, pl.ds(at, half)]


def pack_hidden(core, hidden, half):
    _, rows, width = hidden.shape
    return pl.pallas_call(
        functools.partial(pack_hidden_kernel, half),
        out_shape=jax.ShapeDtypeStruct((rows, width // 2), jnp.bfloat16),
        in_specs=[SMEM, VMEM],
        out_specs=VMEM,
        compiler_params=pltpu.CompilerParams(vmem_limit_bytes=LIMIT),
        name="pack_hidden",
    )(core.reshape(1), hidden)


def project_kernel(half, chunk_ref, hidden_ref, start_ref, *refs):
    weights, out_ref = refs[:-1], refs[-1]
    total = start_ref[...]
    j = 0
    for weight_ref in weights:
        for i in range(weight_ref.shape[0] // half):
            at = pl.multiple_of(chunk_ref[j] * half, half)
            block = weight_ref[i * half : (i + 1) * half, :]
            total += dot(hidden_ref[0, :, pl.ds(at, half)], block, ((1,), (0,)))
            j += 1
    out_ref[...] = total.astype(out_ref.dtype)


def project(chunks, hidden, weights, start, kind):
    half = sum(weight.shape[0] for weight in weights) // len(chunks)
    return pl.pallas_call(
        functools.partial(project_kernel, half),
        out_shape=jax.ShapeDtypeStruct(start.shape, kind),
        in_specs=[SMEM] + [VMEM] * (2 + len(weights)),
        out_specs=VMEM,
        compiler_params=pltpu.CompilerParams(vmem_limit_bytes=LIMIT),
        name="project",
    )(jnp.stack(chunks).astype(jnp.int32), hidden, start, *weights)


def put_scalars(out_ref, at, tails):
    parts = pieces(jnp.sum(tails, axis=0, keepdims=True))
    out_ref[at:, :] = jnp.zeros((PAD, out_ref.shape[1]), out_ref.dtype)
    for i, part in enumerate(parts):
        out_ref[at + i : at + i + 1, :] = part


def grad_kernel(half, core_ref, near_ref, far_ref, hidden_ref, feats_ref, out_ref):
    chips = out_ref.shape[0]
    slab = half // chips
    step = max(slab, 128)
    near, far = [
        [ref[i * BLOCK : (i + 1) * BLOCK, :] for i in range(2)] for ref in (near_ref, far_ref)
    ]
    for f in range(feats_ref.shape[1] // half):
        for at in range(0, half, step):
            mine = pl.multiple_of((2 * f + core_ref[0]) * half + at, step)
            near_feats = hidden_ref[0, :, pl.ds(mine, step)]
            far_feats = feats_ref[:, f * half + at : f * half + at + step]
            turned = sum(dot(part, near_feats, ((0,), (0,))) for part in near)
            turned += sum(dot(part, far_feats, ((0,), (0,))) for part in far)
            turned = turned.T.astype(out_ref.dtype)
            for i in range(step // slab):
                rows = turned[i * slab : (i + 1) * slab]
                out_ref[at // slab + i, f * slab : (f + 1) * slab, :] = rows
    tails = [ref[2 * BLOCK :, :].astype(jnp.float32) for ref in (near_ref, far_ref)]
    for q in range(chips):
        put_scalars(out_ref.at[q], out_ref.shape[1] - PAD, tails[0] + tails[1])


def weight_grad(core, near, far, hidden, feats, half, chips):
    fsdp = feats.shape[1] // half
    rows = fsdp * half // chips + PAD
    return pl.pallas_call(
        functools.partial(grad_kernel, half),
        out_shape=jax.ShapeDtypeStruct((chips, rows, near.shape[1]), jnp.bfloat16),
        in_specs=[SMEM] + [VMEM] * 4,
        out_specs=VMEM,
        compiler_params=pltpu.CompilerParams(vmem_limit_bytes=LIMIT),
        name="weight_grad",
    )(core.reshape(1), near, far, hidden, feats)


def add_chips_kernel(grad_ref, out_ref):
    fsdp, slab = out_ref.shape[0], out_ref.shape[1] - PAD
    total = jnp.sum(grad_ref[...].astype(jnp.float32), axis=0)
    for f in range(fsdp):
        out_ref[f, :slab, :] = total[f * slab : (f + 1) * slab].astype(out_ref.dtype)
        put_scalars(out_ref.at[f], slab, total[fsdp * slab :])


def add_chips(grad, fsdp):
    _, rows, width = grad.shape
    return pl.pallas_call(
        add_chips_kernel,
        out_shape=jax.ShapeDtypeStruct((fsdp, (rows - PAD) // fsdp + PAD, width), jnp.bfloat16),
        in_specs=[VMEM],
        out_specs=VMEM,
        compiler_params=pltpu.CompilerParams(vmem_limit_bytes=LIMIT),
        name="add_chips",
    )(grad)


def add_kernel(grad_ref, out_ref, alog_ref, skip_ref, loss_ref):
    count, slab = grad_ref.shape[0], out_ref.shape[0]
    heads = alog_ref.shape[1]
    total = jnp.sum(grad_ref[...].astype(jnp.float32), axis=0)
    out_ref[...] = total[:slab].astype(out_ref.dtype)
    total = jnp.sum(total[slab:], axis=0, keepdims=True)
    alog_ref[...] = total[:, :heads]
    skip_ref[...] = total[:, heads : 2 * heads]
    loss_ref[...] = total[:, 2 * heads : 2 * heads + 1]


def add_blocks(grad, heads):
    _, rows, width = grad.shape
    return pl.pallas_call(
        add_kernel,
        out_shape=(
            jax.ShapeDtypeStruct((rows - PAD, width), jnp.bfloat16),
            jax.ShapeDtypeStruct((1, heads), jnp.float32),
            jax.ShapeDtypeStruct((1, heads), jnp.float32),
            jax.ShapeDtypeStruct((1, 1), jnp.float32),
        ),
        in_specs=[VMEM],
        out_specs=(VMEM,) * 4,
        compiler_params=pltpu.CompilerParams(vmem_limit_bytes=LIMIT),
        name="add_blocks",
    )(grad)


def finish_kernel(grad_ref, out_ref):
    count = grad_ref.shape[0]
    for q in range(count // 2):
        for r in range(2):
            out_ref[r * (count // 2) + q] = grad_ref[2 * q + r].astype(jnp.float32)


def finish(grad):
    return pl.pallas_call(
        finish_kernel,
        out_shape=jax.ShapeDtypeStruct(grad.shape, jnp.float32),
        in_specs=[VMEM],
        out_specs=VMEM,
        compiler_params=pltpu.CompilerParams(vmem_limit_bytes=LIMIT),
        name="finish",
    )(grad)


def exchange(blocks, axis):
    return lax.all_to_all(blocks, axis, 0, 0, tiled=True)


def swap(block, axis, shift):
    return lax.ppermute(block, axis, [(i, i ^ shift) for i in range(lax.axis_size(axis))])


def local(hidden, values, targets, dt_raw, proj_weight, a_log, skip):
    fsdp, ctx = lax.axis_size("fsdp"), lax.axis_size("ctx")
    mine = lax.axis_index("ctx")
    core = mine % 2
    rows = hidden.shape[1]
    length = rows * ctx
    heads_all = a_log.shape[0]
    inner = values.shape[2]
    cols = inner // ctx
    heads = cols // HDIM
    half = proj_weight.shape[0] // 2
    slab = proj_weight.shape[0] // ctx
    both = proj_weight.shape[1]
    first = mine * heads
    scale = 1.0 / (inner * math.sqrt(fsdp * length))

    shard = lax.axis_index("fsdp")
    others = [shard ^ shift for shift in range(1, fsdp)]

    vt, part = pack_mixer(core, values, targets, dt_raw, proj_weight, ctx)
    near = [swap(part, "fsdp", shift) for shift in range(1, fsdp)]
    vt = exchange(vt, "ctx")
    a_mine = lax.dynamic_slice_in_dim(a_log, first, heads, 0)
    s_mine = lax.dynamic_slice_in_dim(skip, first, heads, 0)
    rates = jnp.tile(-jnp.exp(a_mine), ctx)[:, None]
    send = pack_hidden(1 - core, hidden, half)
    start = jnp.zeros((rows, both), jnp.float32)
    start = project([2 * shard, 2 * shard + 1], hidden, [proj_weight], start, jnp.float32)
    far = [swap(block, "ctx", 1) for block in near]
    far, send, rates, s_mine, start = lax.optimization_barrier((far, send, rates, s_mine, start))

    near_at = [2 * other + core for other in others]
    far_at = [2 * other + 1 - core for other in others]
    chunks = [at[i] for i in range(fsdp - 1) for at in (near_at, far_at)]
    blocks = [part[i] for i in range(fsdp - 1) for part in (near, far)]
    projection = project(chunks, hidden, blocks, start, jnp.bfloat16)
    projection, vt = lax.optimization_barrier((projection, vt))
    maps = lax.all_gather(projection, "ctx", axis=0, tiled=True)
    maps, send = lax.optimization_barrier((maps, send))
    feats = swap(send, "ctx", 1)

    proj_part, packed = mixer(maps, vt, rates, s_mine, first, scale, heads_all)

    proj_part = exchange(proj_part.reshape(ctx, rows, both), "ctx").astype(jnp.float32)
    proj_grad = jnp.sum(proj_part, axis=0)
    high = lax.reduce_precision(proj_grad, 8, 7)
    proj_grad = [part.astype(jnp.bfloat16) for part in (high, proj_grad - high)]
    proj_grad = jnp.concatenate(proj_grad + [packed], axis=0)
    proj_far = swap(proj_grad, "ctx", 1)

    grad = weight_grad(core, proj_grad, proj_far, hidden, feats, half, ctx // 2)
    chips = [list(range(r, ctx, 2)) for r in range(2)]
    grad = lax.all_to_all(grad, "ctx", 0, 0, tiled=True, axis_index_groups=chips)
    grad = exchange(add_chips(grad, fsdp), "fsdp")
    grad, grad_a, grad_skip, loss = add_blocks(grad, heads_all)
    grad_w = finish(lax.all_gather(grad, "ctx", axis=0)).reshape(ctx * slab, both)
    return (grad_w, grad_a.reshape(heads_all), grad_skip.reshape(heads_all), loss.reshape(()))


def solution(mesh):
    in_specs = (
        P("fsdp", "ctx", None),
        P("fsdp", "ctx", None),
        P("fsdp", "ctx", None),
        P("fsdp", None, "ctx"),
        P("fsdp", None),
        P(),
        P(),
    )
    out_specs = (P("fsdp", None), P(), P(), P())
    return jax.shard_map(local, mesh=mesh, in_specs=in_specs, out_specs=out_specs, check_vma=False)
```

```python
import functools
import math

import jax
import jax.numpy as jnp
from jax import lax
from jax.experimental import pallas as pl
from jax.experimental.pallas import tpu as pltpu
from jax.sharding import PartitionSpec as P

BLOCK = 128
HDIM = 128
PAD = 16


def dot(left, right, dims):
    return lax.dot_general(left, right, (dims, ((), ())), preferred_element_type=jnp.float32)


def fold(value):
    return jnp.sum(value.reshape(value.shape[0] // 8, 8, value.shape[1]), axis=0)


def pieces(value):
    high = value.astype(jnp.bfloat16)
    rest = value - high.astype(jnp.float32)
    middle = rest.astype(jnp.bfloat16)
    return high, middle, (rest - middle.astype(jnp.float32)).astype(jnp.bfloat16)


def running_sum(value):
    lane = lax.broadcasted_iota(jnp.int32, value.shape, 1)
    shift = 1
    while shift < value.shape[1]:
        value += jnp.where(lane >= shift, pltpu.roll(value, shift, 1), 0.0)
        shift *= 2
    return value


def softplus(value):
    small = jnp.exp(-jnp.abs(value))
    series = small * (1.0 - small * (0.5 - small * (1 / 3 - small * (0.25 - small * 0.2))))
    return jnp.maximum(value, 0.0) + jnp.where(small < 0.03, series, jnp.log1p(small))


def mixer_kernel(
    heads, scale, count, maps_ref, vt_hbm, rate_ref, skip_ref, first_ref, out_ref, pack_ref,
    vt_ref, rows_ref, cols_ref, carry_ref, last_ref, states, entries, parts, stat_ref, sems,
):
    blocks, tail_at, width = vt_ref.shape[0], vt_ref.shape[1] - PAD, vt_ref.shape[2]
    half = maps_ref.shape[1] // 2
    full = heads * width
    tail = pltpu.make_async_copy(
        vt_hbm.at[:, pl.ds(tail_at, PAD)], vt_ref.at[:, pl.ds(tail_at, PAD)], sems.at[blocks]
    )
    tail.start()

    def load(k):
        body = pl.ds(0, tail_at)
        return pltpu.make_async_copy(vt_hbm.at[k, body], vt_ref.at[k, body], sems.at[k])

    for k in range(blocks):
        load(k).start()
    stat_ref[...] = jnp.zeros_like(stat_ref)
    t_at = lax.broadcasted_iota(jnp.int32, (BLOCK, BLOCK), 0)
    s_at = lax.broadcasted_iota(jnp.int32, (BLOCK, BLOCK), 1)
    mask = t_at >= s_at
    tail.wait()
    sent = []
    for k in range(blocks):
        rows = vt_ref[k, tail_at:, :].astype(jnp.float32)
        sent.append(rows[:heads] + rows[heads : 2 * heads] + rows[2 * heads : 3 * heads])
    step = softplus(jnp.concatenate(sent, axis=0))
    decay = running_sum(step * rate_ref[...])
    final = decay[:, BLOCK - 1 :]
    growth = jnp.exp(decay)
    tails = final - decay
    made = (growth, growth * decay, jnp.exp(tails) * step, tails, decay, step)
    carry = jnp.broadcast_to(jnp.exp(final), (blocks * heads, width))
    last = jnp.broadcast_to(jnp.exp(final) * final, (blocks * heads, width))
    for k in range(blocks):
        own = slice(k * heads, (k + 1) * heads)
        rows_ref[k] = jnp.concatenate([x[own, :] for x in made], axis=0)
        for h in range(heads):
            one = slice(k * heads + h, k * heads + h + 1)
            carry_ref[k, :, h * width : (h + 1) * width] = carry[one, :]
            last_ref[k, :, h * width : (h + 1) * width] = last[one, :]

    def forward(k, state):
        load(k).wait()
        at = pl.ds(pl.multiple_of(k * BLOCK, BLOCK), BLOCK)
        maps, rows = maps_ref[at, :], rows_ref[k]
        cols = rows.T
        cols_ref[k] = cols
        b, c = maps[:, :half], maps[:, half:]
        scores = dot(c, b, ((1,), (1,)))
        state_bf = state.astype(jnp.bfloat16)
        states[k] = state
        from_all = dot(c, state_bf, ((1,), (0,)))
        score_grad = jnp.zeros((BLOCK, BLOCK), jnp.float32)
        grown, weighed = [], []
        for h in range(heads):
            col = lambda j: cols[:, j * heads + h : j * heads + h + 1]
            v = vt_ref[k, h * BLOCK : (h + 1) * BLOCK, :]
            goal = vt_ref[k, (heads + h) * BLOCK : (heads + h + 1) * BLOCK, :]
            vf = v.astype(jnp.float32)
            row = lambda j: rows[j * heads + h : j * heads + h + 1, :]
            diff = jnp.minimum(col(4) - row(4), 0.0)
            within = jnp.where(mask, jnp.exp(diff), 0.0) * row(5)
            mixing = within * scores
            inner = dot(mixing.astype(jnp.bfloat16), v, ((1,), (0,)))
            from_state = from_all[:, h * width : (h + 1) * width]
            growth = col(0)
            out = inner + growth * from_state + skip_ref[h] * vf
            misfit = out - goal.astype(jnp.float32)
            grad = misfit * scale
            mix_grad = dot(grad.astype(jnp.bfloat16), v, ((1,), (1,)))
            grown.append((grad * growth).astype(jnp.bfloat16))
            weighed.append((vf * col(2)).astype(jnp.bfloat16))
            stat_ref[h, 0] += fold(misfit * misfit)
            stat_ref[h, 1] += fold(grad * vf)
            stat_ref[h, 2] += fold(grad * from_state * col(1))
            score_grad += within * mix_grad
            stat_ref[h, 2] += fold(mix_grad * mixing * diff)
        grown = jnp.concatenate(grown, axis=1)
        weighed = jnp.concatenate(weighed, axis=1)
        entries[k] = dot(c, grown, ((0,), (0,)))
        score_bf = score_grad.astype(jnp.bfloat16)
        grad_c = dot(grown, state_bf, ((1,), (1,))) + dot(score_bf, b, ((1,), (0,)))
        grad_b = dot(score_bf, c, ((0,), (0,)))
        parts[at, :] = jnp.concatenate([grad_b, grad_c], axis=1)
        return carry_ref[k] * state + dot(b, weighed, ((0,), (0,)))

    unrolled(blocks, forward, jnp.zeros((half, full), jnp.float32))

    def backward(i, leaving):
        k = blocks - 1 - i
        at = pl.ds(pl.multiple_of(k * BLOCK, BLOCK), BLOCK)
        bf = maps_ref[at, :][:, :half].astype(jnp.float32)
        cols = cols_ref[k]
        leaving_bf = leaving.astype(jnp.bfloat16)
        grad_b = jnp.zeros((BLOCK, half), jnp.float32)
        overlap = leaving * states[k] * last_ref[k]
        for h in range(heads):
            piece = slice(h * width, (h + 1) * width)
            v = vt_ref[k, h * BLOCK : (h + 1) * BLOCK, :]
            coef_grad = dot(v, leaving_bf[:, piece], ((1,), (1,)))
            pulled = coef_grad * cols[:, 2 * heads + h : 2 * heads + h + 1]
            grad_b += pulled
            tail_w = cols[:, 3 * heads + h : 3 * heads + h + 1]
            stat_ref[h, 2, :, :half] += fold(pulled * bf * tail_w)
            stat_ref[h, 2] += fold(overlap[:, piece])
        both = jnp.concatenate([grad_b, jnp.zeros_like(grad_b)], axis=1)
        out_ref[at, :] = (parts[at, :] + both).astype(out_ref.dtype)
        return entries[k] + carry_ref[k] * leaving

    unrolled(blocks, backward, jnp.zeros((half, full), jnp.float32))

    lane = lax.broadcasted_iota(jnp.int32, (1, 128), 1)
    packed = jnp.zeros((1, 128), jnp.float32)
    for h in range(heads):
        at_head = first_ref[0] + h
        sums = [jnp.sum(stat_ref[h, i]) for i in range(3)]
        packed += jnp.where(lane == at_head, sums[2], 0.0)
        packed += jnp.where(lane == count + at_head, sums[1], 0.0)
        packed += jnp.where(lane == 2 * count, 0.5 * scale * sums[0], 0.0)
    pack_ref[...] = jnp.zeros_like(pack_ref)
    for i, piece in enumerate(pieces(packed)):
        pack_ref[i : i + 1, :] = piece


def unrolled(count, step, start):
    each = 4 if count % 4 == 0 else 1

    def several(i, value):
        for j in range(each):
            value = step(i * each + j, value)
        return value

    return lax.fori_loop(0, count // each, several, start)


VMEM = pl.BlockSpec(memory_space=pltpu.VMEM)
SMEM = pl.BlockSpec(memory_space=pltpu.SMEM)
ANY = pl.BlockSpec(memory_space=pl.ANY)
LIMIT = 28 * 1024 * 1024


def mixer(maps, vt, rates, skip, first, scale, count):
    blocks, rows, width = vt.shape
    length, both = maps.shape
    heads = (rows - PAD) // BLOCK // 2
    full = heads * width
    return pl.pallas_call(
        functools.partial(mixer_kernel, heads, scale, count),
        out_shape=(
            jax.ShapeDtypeStruct((length, both), jnp.bfloat16),
            jax.ShapeDtypeStruct((PAD, 128), jnp.bfloat16),
        ),
        in_specs=[VMEM, ANY, VMEM, SMEM, SMEM],
        out_specs=(VMEM, VMEM),
        scratch_shapes=[
            pltpu.VMEM((blocks, rows, width), jnp.bfloat16),
            pltpu.VMEM((blocks, 6 * heads, BLOCK), jnp.float32),
            pltpu.VMEM((blocks, BLOCK, 6 * heads), jnp.float32),
            pltpu.VMEM((blocks, 1, full), jnp.float32),
            pltpu.VMEM((blocks, 1, full), jnp.float32),
            pltpu.VMEM((blocks, both // 2, full), jnp.float32),
            pltpu.VMEM((blocks, both // 2, full), jnp.float32),
            pltpu.VMEM((length, both), jnp.float32),
            pltpu.VMEM((heads, 3, 8, 128), jnp.float32),
            pltpu.SemaphoreType.DMA((blocks + 1,)),
        ],
        compiler_params=pltpu.CompilerParams(vmem_limit_bytes=LIMIT),
        cost_estimate=pl.CostEstimate(
            flops=14 * length * BLOCK * full, bytes_accessed=6 * length * full, transcendentals=0
        ),
        name="mixer",
    )(maps, vt, rates, skip, first.reshape(1))


def pack_mixer_kernel(
    core_ref, values_hbm, targets_hbm, dt_ref, weight_hbm, out_hbm, part_ref, held, out_ref,
    weight_sem, in_sems, sems,
):
    count, rows, width = out_ref.shape
    heads = (rows - PAD) // BLOCK // 2
    loads = []
    for c in range(count):
        own = pl.ds(c * heads * width, heads * width)
        for i, ref in enumerate((values_hbm, targets_hbm)):
            copy = pltpu.make_async_copy(ref.at[0, :, own], held.at[c, i], in_sems.at[c, i])
            copy.start()
            loads.append(copy)
    half = part_ref.shape[0]
    at = pl.multiple_of(core_ref[0] * half, half)
    load = pltpu.make_async_copy(weight_hbm.at[pl.ds(at, half), :], part_ref, weight_sem)
    load.start()
    for c in range(count):
        sent = [x.astype(jnp.float32) for x in pieces(dt_ref[0, c * heads : (c + 1) * heads, :])]
        sent.append(jnp.zeros((PAD - 3 * heads, width), jnp.float32))
        out_ref[c, rows - PAD :, :] = jnp.concatenate(sent, axis=0).astype(jnp.bfloat16)
    stores = []
    for c in range(count):
        for i in range(2):
            loads[2 * c + i].wait()
            for h in range(heads):
                to = (i * heads + h) * BLOCK
                out_ref[c, to : to + BLOCK, :] = held[c, i, :, h * width : (h + 1) * width]
        stores.append(pltpu.make_async_copy(out_ref.at[c], out_hbm.at[c], sems.at[c]))
        stores[c].start()
    load.wait()
    for copy in stores:
        copy.wait()


def pack_mixer(core, values, targets, dt_raw, weight, ctx):
    rows, width = values.shape[1:]
    heads = dt_raw.shape[1] // ctx
    shape = (ctx, 2 * heads * BLOCK + PAD, HDIM)
    return pl.pallas_call(
        pack_mixer_kernel,
        out_shape=(
            jax.ShapeDtypeStruct(shape, jnp.bfloat16),
            jax.ShapeDtypeStruct((weight.shape[0] // 2, weight.shape[1]), jnp.bfloat16),
        ),
        in_specs=[SMEM, ANY, ANY, VMEM, ANY],
        out_specs=(ANY, VMEM),
        scratch_shapes=[
            pltpu.VMEM((ctx, 2, rows, width // ctx), jnp.bfloat16),
            pltpu.VMEM(shape, jnp.bfloat16),
            pltpu.SemaphoreType.DMA,
            pltpu.SemaphoreType.DMA((ctx, 2)),
            pltpu.SemaphoreType.DMA((ctx,)),
        ],
        name="pack_mixer",
    )(core.reshape(1), values, targets, dt_raw, weight)


def pack_hidden_kernel(half, core_ref, hidden_ref, out_ref):
    for f in range(out_ref.shape[1] // half):
        at = pl.multiple_of((2 * f + core_ref[0]) * half, half)
        out_ref[:, f * half : (f + 1) * half] = hidden_ref[0, :, pl.ds(at, half)]


def pack_hidden(core, hidden, half):
    _, rows, width = hidden.shape
    return pl.pallas_call(
        functools.partial(pack_hidden_kernel, half),
        out_shape=jax.ShapeDtypeStruct((rows, width // 2), jnp.bfloat16),
        in_specs=[SMEM, VMEM],
        out_specs=VMEM,
        compiler_params=pltpu.CompilerParams(vmem_limit_bytes=LIMIT),
        name="pack_hidden",
    )(core.reshape(1), hidden)


def project_kernel(half, chunk_ref, hidden_ref, start_ref, *refs):
    weights, out_ref = refs[:-1], refs[-1]
    total = start_ref[...]
    j = 0
    for weight_ref in weights:
        for i in range(weight_ref.shape[0] // half):
            at = pl.multiple_of(chunk_ref[j] * half, half)
            block = weight_ref[i * half : (i + 1) * half, :]
            total += dot(hidden_ref[0, :, pl.ds(at, half)], block, ((1,), (0,)))
            j += 1
    out_ref[...] = total.astype(out_ref.dtype)


def project(chunks, hidden, weights, start, kind):
    half = sum(weight.shape[0] for weight in weights) // len(chunks)
    return pl.pallas_call(
        functools.partial(project_kernel, half),
        out_shape=jax.ShapeDtypeStruct(start.shape, kind),
        in_specs=[SMEM] + [VMEM] * (2 + len(weights)),
        out_specs=VMEM,
        compiler_params=pltpu.CompilerParams(vmem_limit_bytes=LIMIT),
        name="project",
    )(jnp.stack(chunks).astype(jnp.int32), hidden, start, *weights)


def put_scalars(out_ref, at, tails):
    parts = pieces(jnp.sum(tails, axis=0, keepdims=True))
    out_ref[at:, :] = jnp.zeros((PAD, out_ref.shape[1]), out_ref.dtype)
    for i, part in enumerate(parts):
        out_ref[at + i : at + i + 1, :] = part


def grad_kernel(half, core_ref, near_ref, far_ref, hidden_ref, feats_ref, out_ref):
    chips = out_ref.shape[0]
    slab = half // chips
    step = max(slab, 128)
    near, far = [
        [ref[i * BLOCK : (i + 1) * BLOCK, :] for i in range(2)] for ref in (near_ref, far_ref)
    ]
    for f in range(feats_ref.shape[1] // half):
        for at in range(0, half, step):
            mine = pl.multiple_of((2 * f + core_ref[0]) * half + at, step)
            near_feats = hidden_ref[0, :, pl.ds(mine, step)]
            far_feats = feats_ref[:, f * half + at : f * half + at + step]
            turned = sum(dot(part, near_feats, ((0,), (0,))) for part in near)
            turned += sum(dot(part, far_feats, ((0,), (0,))) for part in far)
            turned = turned.T.astype(out_ref.dtype)
            for i in range(step // slab):
                rows = turned[i * slab : (i + 1) * slab]
                out_ref[at // slab + i, f * slab : (f + 1) * slab, :] = rows
    tails = [ref[2 * BLOCK :, :].astype(jnp.float32) for ref in (near_ref, far_ref)]
    for q in range(chips):
        put_scalars(out_ref.at[q], out_ref.shape[1] - PAD, tails[0] + tails[1])


def weight_grad(core, near, far, hidden, feats, half, chips):
    fsdp = feats.shape[1] // half
    rows = fsdp * half // chips + PAD
    return pl.pallas_call(
        functools.partial(grad_kernel, half),
        out_shape=jax.ShapeDtypeStruct((chips, rows, near.shape[1]), jnp.bfloat16),
        in_specs=[SMEM] + [VMEM] * 4,
        out_specs=VMEM,
        compiler_params=pltpu.CompilerParams(vmem_limit_bytes=LIMIT),
        name="weight_grad",
    )(core.reshape(1), near, far, hidden, feats)


def add_chips_kernel(grad_ref, out_ref):
    fsdp, slab = out_ref.shape[0], out_ref.shape[1] - PAD
    total = jnp.sum(grad_ref[...].astype(jnp.float32), axis=0)
    for f in range(fsdp):
        out_ref[f, :slab, :] = total[f * slab : (f + 1) * slab].astype(out_ref.dtype)
        put_scalars(out_ref.at[f], slab, total[fsdp * slab :])


def add_chips(grad, fsdp):
    _, rows, width = grad.shape
    return pl.pallas_call(
        add_chips_kernel,
        out_shape=jax.ShapeDtypeStruct((fsdp, (rows - PAD) // fsdp + PAD, width), jnp.bfloat16),
        in_specs=[VMEM],
        out_specs=VMEM,
        compiler_params=pltpu.CompilerParams(vmem_limit_bytes=LIMIT),
        name="add_chips",
    )(grad)


def add_kernel(grad_ref, out_ref, alog_ref, skip_ref, loss_ref):
    count, slab = grad_ref.shape[0], out_ref.shape[0]
    heads = alog_ref.shape[1]
    total = jnp.sum(grad_ref[...].astype(jnp.float32), axis=0)
    out_ref[...] = total[:slab].astype(out_ref.dtype)
    total = jnp.sum(total[slab:], axis=0, keepdims=True)
    alog_ref[...] = total[:, :heads]
    skip_ref[...] = total[:, heads : 2 * heads]
    loss_ref[...] = total[:, 2 * heads : 2 * heads + 1]


def add_blocks(grad, heads):
    _, rows, width = grad.shape
    return pl.pallas_call(
        add_kernel,
        out_shape=(
            jax.ShapeDtypeStruct((rows - PAD, width), jnp.bfloat16),
            jax.ShapeDtypeStruct((1, heads), jnp.float32),
            jax.ShapeDtypeStruct((1, heads), jnp.float32),
            jax.ShapeDtypeStruct((1, 1), jnp.float32),
        ),
        in_specs=[VMEM],
        out_specs=(VMEM,) * 4,
        compiler_params=pltpu.CompilerParams(vmem_limit_bytes=LIMIT),
        name="add_blocks",
    )(grad)


def finish_kernel(grad_ref, out_ref):
    count = grad_ref.shape[0]
    for q in range(count // 2):
        for r in range(2):
            out_ref[r * (count // 2) + q] = grad_ref[2 * q + r].astype(jnp.float32)


def finish(grad):
    return pl.pallas_call(
        finish_kernel,
        out_shape=jax.ShapeDtypeStruct(grad.shape, jnp.float32),
        in_specs=[VMEM],
        out_specs=VMEM,
        compiler_params=pltpu.CompilerParams(vmem_limit_bytes=LIMIT),
        name="finish",
    )(grad)


def exchange(blocks, axis):
    return lax.all_to_all(blocks, axis, 0, 0, tiled=True)


def swap(block, axis, shift):
    return lax.ppermute(block, axis, [(i, i ^ shift) for i in range(lax.axis_size(axis))])


def local(hidden, values, targets, dt_raw, proj_weight, a_log, skip):
    fsdp, ctx = lax.axis_size("fsdp"), lax.axis_size("ctx")
    mine = lax.axis_index("ctx")
    core = mine % 2
    rows = hidden.shape[1]
    length = rows * ctx
    heads_all = a_log.shape[0]
    inner = values.shape[2]
    cols = inner // ctx
    heads = cols // HDIM
    half = proj_weight.shape[0] // 2
    slab = proj_weight.shape[0] // ctx
    both = proj_weight.shape[1]
    first = mine * heads
    scale = 1.0 / (inner * math.sqrt(fsdp * length))

    shard = lax.axis_index("fsdp")
    others = [shard ^ shift for shift in range(1, fsdp)]

    vt, part = pack_mixer(core, values, targets, dt_raw, proj_weight, ctx)
    near = [swap(part, "fsdp", shift) for shift in range(1, fsdp)]
    vt = exchange(vt, "ctx")
    a_mine = lax.dynamic_slice_in_dim(a_log, first, heads, 0)
    s_mine = lax.dynamic_slice_in_dim(skip, first, heads, 0)
    rates = jnp.tile(-jnp.exp(a_mine), ctx)[:, None]
    send = pack_hidden(1 - core, hidden, half)
    start = jnp.zeros((rows, both), jnp.float32)
    start = project([2 * shard, 2 * shard + 1], hidden, [proj_weight], start, jnp.float32)
    near[0], send, rates, s_mine, start = lax.optimization_barrier(
        (near[0], send, rates, s_mine, start)
    )
    far = [swap(block, "ctx", 1) for block in near]

    near_at = [2 * other + core for other in others]
    far_at = [2 * other + 1 - core for other in others]
    chunks = [at[i] for i in range(fsdp - 1) for at in (near_at, far_at)]
    blocks = [part[i] for i in range(fsdp - 1) for part in (near, far)]
    projection = project(chunks, hidden, blocks, start, jnp.bfloat16)
    projection, vt = lax.optimization_barrier((projection, vt))
    maps = lax.all_gather(projection, "ctx", axis=0, tiled=True)
    maps, send = lax.optimization_barrier((maps, send))
    feats = swap(send, "ctx", 1)

    proj_part, packed = mixer(maps, vt, rates, s_mine, first, scale, heads_all)

    proj_part = exchange(proj_part.reshape(ctx, rows, both), "ctx").astype(jnp.float32)
    proj_grad = jnp.sum(proj_part, axis=0)
    high = lax.reduce_precision(proj_grad, 8, 7)
    proj_grad = [part.astype(jnp.bfloat16) for part in (high, proj_grad - high)]
    proj_grad = jnp.concatenate(proj_grad + [packed], axis=0)
    proj_far = swap(proj_grad, "ctx", 1)

    grad = weight_grad(core, proj_grad, proj_far, hidden, feats, half, ctx // 2)
    chips = [list(range(r, ctx, 2)) for r in range(2)]
    grad = lax.all_to_all(grad, "ctx", 0, 0, tiled=True, axis_index_groups=chips)
    grad = exchange(add_chips(grad, fsdp), "fsdp")
    grad, grad_a, grad_skip, loss = add_blocks(grad, heads_all)
    grad_w = finish(lax.all_gather(grad, "ctx", axis=0)).reshape(ctx * slab, both)
    return (grad_w, grad_a.reshape(heads_all), grad_skip.reshape(heads_all), loss.reshape(()))


def solution(mesh):
    in_specs = (
        P("fsdp", "ctx", None),
        P("fsdp", "ctx", None),
        P("fsdp", "ctx", None),
        P("fsdp", None, "ctx"),
        P("fsdp", None),
        P(),
        P(),
    )
    out_specs = (P("fsdp", None), P(), P(), P())
    return jax.shard_map(local, mesh=mesh, in_specs=in_specs, out_specs=out_specs, check_vma=False)
```

```python
import functools
import math

import jax
import jax.numpy as jnp
from jax import lax
from jax.experimental import pallas as pl
from jax.experimental.pallas import tpu as pltpu
from jax.sharding import PartitionSpec as P

BLOCK = 128
HDIM = 128
PAD = 16


def dot(left, right, dims):
    return lax.dot_general(left, right, (dims, ((), ())), preferred_element_type=jnp.float32)


def fold(value):
    return jnp.sum(value.reshape(value.shape[0] // 8, 8, value.shape[1]), axis=0)


def pieces(value):
    high = value.astype(jnp.bfloat16)
    rest = value - high.astype(jnp.float32)
    middle = rest.astype(jnp.bfloat16)
    return high, middle, (rest - middle.astype(jnp.float32)).astype(jnp.bfloat16)


def running_sum(value):
    lane = lax.broadcasted_iota(jnp.int32, value.shape, 1)
    shift = 1
    while shift < value.shape[1]:
        value += jnp.where(lane >= shift, pltpu.roll(value, shift, 1), 0.0)
        shift *= 2
    return value


def softplus(value):
    small = jnp.exp(-jnp.abs(value))
    series = small * (1.0 - small * (0.5 - small * (1 / 3 - small * (0.25 - small * 0.2))))
    return jnp.maximum(value, 0.0) + jnp.where(small < 0.03, series, jnp.log1p(small))


def mixer_kernel(
    heads, scale, count, maps_ref, vt_hbm, rate_ref, skip_ref, first_ref, out_ref, pack_ref,
    vt_ref, rows_ref, cols_ref, carry_ref, last_ref, states, entries, parts, stat_ref, sems,
):
    blocks, tail_at, width = vt_ref.shape[0], vt_ref.shape[1] - PAD, vt_ref.shape[2]
    half = maps_ref.shape[1] // 2
    full = heads * width
    tail = pltpu.make_async_copy(
        vt_hbm.at[:, pl.ds(tail_at, PAD)], vt_ref.at[:, pl.ds(tail_at, PAD)], sems.at[blocks]
    )
    tail.start()

    def load(k):
        body = pl.ds(0, tail_at)
        return pltpu.make_async_copy(vt_hbm.at[k, body], vt_ref.at[k, body], sems.at[k])

    for k in range(blocks):
        load(k).start()
    stat_ref[...] = jnp.zeros_like(stat_ref)
    t_at = lax.broadcasted_iota(jnp.int32, (BLOCK, BLOCK), 0)
    s_at = lax.broadcasted_iota(jnp.int32, (BLOCK, BLOCK), 1)
    mask = t_at >= s_at
    tail.wait()
    sent = []
    for k in range(blocks):
        rows = vt_ref[k, tail_at:, :].astype(jnp.float32)
        sent.append(rows[:heads] + rows[heads : 2 * heads] + rows[2 * heads : 3 * heads])
    step = softplus(jnp.concatenate(sent, axis=0))
    decay = running_sum(step * rate_ref[...])
    final = decay[:, BLOCK - 1 :]
    growth = jnp.exp(decay)
    tails = final - decay
    made = (growth, growth * decay, jnp.exp(tails) * step, tails, decay, step)
    carry = jnp.broadcast_to(jnp.exp(final), (blocks * heads, width))
    last = jnp.broadcast_to(jnp.exp(final) * final, (blocks * heads, width))
    for k in range(blocks):
        own = slice(k * heads, (k + 1) * heads)
        rows_ref[k] = jnp.concatenate([x[own, :] for x in made], axis=0)
        for h in range(heads):
            one = slice(k * heads + h, k * heads + h + 1)
            carry_ref[k, :, h * width : (h + 1) * width] = carry[one, :]
            last_ref[k, :, h * width : (h + 1) * width] = last[one, :]

    def forward(k, state):
        load(k).wait()
        at = pl.ds(pl.multiple_of(k * BLOCK, BLOCK), BLOCK)
        maps, rows = maps_ref[at, :], rows_ref[k]
        cols = rows.T
        cols_ref[k] = cols
        b, c = maps[:, :half], maps[:, half:]
        scores = dot(c, b, ((1,), (1,)))
        state_bf = state.astype(jnp.bfloat16)
        states[k] = state
        from_all = dot(c, state_bf, ((1,), (0,)))
        score_grad = jnp.zeros((BLOCK, BLOCK), jnp.float32)
        grown, weighed = [], []
        for h in range(heads):
            col = lambda j: cols[:, j * heads + h : j * heads + h + 1]
            v = vt_ref[k, h * BLOCK : (h + 1) * BLOCK, :]
            goal = vt_ref[k, (heads + h) * BLOCK : (heads + h + 1) * BLOCK, :]
            vf = v.astype(jnp.float32)
            row = lambda j: rows[j * heads + h : j * heads + h + 1, :]
            diff = jnp.minimum(col(4) - row(4), 0.0)
            within = jnp.where(mask, jnp.exp(diff), 0.0) * row(5)
            mixing = within * scores
            inner = dot(mixing.astype(jnp.bfloat16), v, ((1,), (0,)))
            from_state = from_all[:, h * width : (h + 1) * width]
            growth = col(0)
            out = inner + growth * from_state + skip_ref[h] * vf
            misfit = out - goal.astype(jnp.float32)
            grad = misfit * scale
            mix_grad = dot(grad.astype(jnp.bfloat16), v, ((1,), (1,)))
            grown.append((grad * growth).astype(jnp.bfloat16))
            weighed.append((vf * col(2)).astype(jnp.bfloat16))
            stat_ref[h, 0] += fold(misfit * misfit)
            stat_ref[h, 1] += fold(grad * vf)
            stat_ref[h, 2] += fold(grad * from_state * col(1))
            score_grad += within * mix_grad
            stat_ref[h, 2] += fold(mix_grad * mixing * diff)
        grown = jnp.concatenate(grown, axis=1)
        weighed = jnp.concatenate(weighed, axis=1)
        entries[k] = dot(c, grown, ((0,), (0,)))
        score_bf = score_grad.astype(jnp.bfloat16)
        grad_c = dot(grown, state_bf, ((1,), (1,))) + dot(score_bf, b, ((1,), (0,)))
        grad_b = dot(score_bf, c, ((0,), (0,)))
        parts[at, :] = jnp.concatenate([grad_b, grad_c], axis=1)
        return carry_ref[k] * state + dot(b, weighed, ((0,), (0,)))

    unrolled(blocks, forward, jnp.zeros((half, full), jnp.float32))

    def backward(i, leaving):
        k = blocks - 1 - i
        at = pl.ds(pl.multiple_of(k * BLOCK, BLOCK), BLOCK)
        bf = maps_ref[at, :][:, :half].astype(jnp.float32)
        cols = cols_ref[k]
        leaving_bf = leaving.astype(jnp.bfloat16)
        grad_b = jnp.zeros((BLOCK, half), jnp.float32)
        overlap = leaving * states[k] * last_ref[k]
        for h in range(heads):
            piece = slice(h * width, (h + 1) * width)
            v = vt_ref[k, h * BLOCK : (h + 1) * BLOCK, :]
            coef_grad = dot(v, leaving_bf[:, piece], ((1,), (1,)))
            pulled = coef_grad * cols[:, 2 * heads + h : 2 * heads + h + 1]
            grad_b += pulled
            tail_w = cols[:, 3 * heads + h : 3 * heads + h + 1]
            stat_ref[h, 2, :, :half] += fold(pulled * bf * tail_w)
            stat_ref[h, 2] += fold(overlap[:, piece])
        both = jnp.concatenate([grad_b, jnp.zeros_like(grad_b)], axis=1)
        out_ref[at, :] = (parts[at, :] + both).astype(out_ref.dtype)
        return entries[k] + carry_ref[k] * leaving

    unrolled(blocks, backward, jnp.zeros((half, full), jnp.float32))

    lane = lax.broadcasted_iota(jnp.int32, (1, 128), 1)
    packed = jnp.zeros((1, 128), jnp.float32)
    for h in range(heads):
        at_head = first_ref[0] + h
        sums = [jnp.sum(stat_ref[h, i]) for i in range(3)]
        packed += jnp.where(lane == at_head, sums[2], 0.0)
        packed += jnp.where(lane == count + at_head, sums[1], 0.0)
        packed += jnp.where(lane == 2 * count, 0.5 * scale * sums[0], 0.0)
    pack_ref[...] = jnp.zeros_like(pack_ref)
    for i, piece in enumerate(pieces(packed)):
        pack_ref[i : i + 1, :] = piece


def unrolled(count, step, start):
    each = 2 if count % 2 == 0 else 1

    def several(i, value):
        for j in range(each):
            value = step(i * each + j, value)
        return value

    return lax.fori_loop(0, count // each, several, start)


VMEM = pl.BlockSpec(memory_space=pltpu.VMEM)
SMEM = pl.BlockSpec(memory_space=pltpu.SMEM)
ANY = pl.BlockSpec(memory_space=pl.ANY)
LIMIT = 28 * 1024 * 1024


def mixer(maps, vt, rates, skip, first, scale, count):
    blocks, rows, width = vt.shape
    length, both = maps.shape
    heads = (rows - PAD) // BLOCK // 2
    full = heads * width
    return pl.pallas_call(
        functools.partial(mixer_kernel, heads, scale, count),
        out_shape=(
            jax.ShapeDtypeStruct((length, both), jnp.bfloat16),
            jax.ShapeDtypeStruct((PAD, 128), jnp.bfloat16),
        ),
        in_specs=[VMEM, ANY, VMEM, SMEM, SMEM],
        out_specs=(VMEM, VMEM),
        scratch_shapes=[
            pltpu.VMEM((blocks, rows, width), jnp.bfloat16),
            pltpu.VMEM((blocks, 6 * heads, BLOCK), jnp.float32),
            pltpu.VMEM((blocks, BLOCK, 6 * heads), jnp.float32),
            pltpu.VMEM((blocks, 1, full), jnp.float32),
            pltpu.VMEM((blocks, 1, full), jnp.float32),
            pltpu.VMEM((blocks, both // 2, full), jnp.float32),
            pltpu.VMEM((blocks, both // 2, full), jnp.float32),
            pltpu.VMEM((length, both), jnp.float32),
            pltpu.VMEM((heads, 3, 8, 128), jnp.float32),
            pltpu.SemaphoreType.DMA((blocks + 1,)),
        ],
        compiler_params=pltpu.CompilerParams(vmem_limit_bytes=LIMIT),
        cost_estimate=pl.CostEstimate(
            flops=14 * length * BLOCK * full, bytes_accessed=6 * length * full, transcendentals=0
        ),
        name="mixer",
    )(maps, vt, rates, skip, first.reshape(1))


def pack_mixer_kernel(
    core_ref, values_hbm, targets_hbm, dt_ref, weight_hbm, out_hbm, part_ref, held, out_ref,
    weight_sem, in_sems, sems,
):
    count, rows, width = out_ref.shape
    heads = (rows - PAD) // BLOCK // 2
    loads = []
    for c in range(count):
        own = pl.ds(c * heads * width, heads * width)
        for i, ref in enumerate((values_hbm, targets_hbm)):
            copy = pltpu.make_async_copy(ref.at[0, :, own], held.at[c, i], in_sems.at[c, i])
            copy.start()
            loads.append(copy)
    half = part_ref.shape[0]
    at = pl.multiple_of(core_ref[0] * half, half)
    load = pltpu.make_async_copy(weight_hbm.at[pl.ds(at, half), :], part_ref, weight_sem)
    load.start()
    for c in range(count):
        sent = [x.astype(jnp.float32) for x in pieces(dt_ref[0, c * heads : (c + 1) * heads, :])]
        sent.append(jnp.zeros((PAD - 3 * heads, width), jnp.float32))
        out_ref[c, rows - PAD :, :] = jnp.concatenate(sent, axis=0).astype(jnp.bfloat16)
    stores = []
    for c in range(count):
        for i in range(2):
            loads[2 * c + i].wait()
            for h in range(heads):
                to = (i * heads + h) * BLOCK
                out_ref[c, to : to + BLOCK, :] = held[c, i, :, h * width : (h + 1) * width]
        stores.append(pltpu.make_async_copy(out_ref.at[c], out_hbm.at[c], sems.at[c]))
        stores[c].start()
    load.wait()
    for copy in stores:
        copy.wait()


def pack_mixer(core, values, targets, dt_raw, weight, ctx):
    rows, width = values.shape[1:]
    heads = dt_raw.shape[1] // ctx
    shape = (ctx, 2 * heads * BLOCK + PAD, HDIM)
    return pl.pallas_call(
        pack_mixer_kernel,
        out_shape=(
            jax.ShapeDtypeStruct(shape, jnp.bfloat16),
            jax.ShapeDtypeStruct((weight.shape[0] // 2, weight.shape[1]), jnp.bfloat16),
        ),
        in_specs=[SMEM, ANY, ANY, VMEM, ANY],
        out_specs=(ANY, VMEM),
        scratch_shapes=[
            pltpu.VMEM((ctx, 2, rows, width // ctx), jnp.bfloat16),
            pltpu.VMEM(shape, jnp.bfloat16),
            pltpu.SemaphoreType.DMA,
            pltpu.SemaphoreType.DMA((ctx, 2)),
            pltpu.SemaphoreType.DMA((ctx,)),
        ],
        name="pack_mixer",
    )(core.reshape(1), values, targets, dt_raw, weight)


def pack_hidden_kernel(half, core_ref, hidden_ref, out_ref):
    for f in range(out_ref.shape[1] // half):
        at = pl.multiple_of((2 * f + core_ref[0]) * half, half)
        out_ref[:, f * half : (f + 1) * half] = hidden_ref[0, :, pl.ds(at, half)]


def pack_hidden(core, hidden, half):
    _, rows, width = hidden.shape
    return pl.pallas_call(
        functools.partial(pack_hidden_kernel, half),
        out_shape=jax.ShapeDtypeStruct((rows, width // 2), jnp.bfloat16),
        in_specs=[SMEM, VMEM],
        out_specs=VMEM,
        compiler_params=pltpu.CompilerParams(vmem_limit_bytes=LIMIT),
        name="pack_hidden",
    )(core.reshape(1), hidden)


def project_kernel(half, chunk_ref, hidden_ref, start_ref, *refs):
    weights, out_ref = refs[:-1], refs[-1]
    total = start_ref[...]
    j = 0
    for weight_ref in weights:
        for i in range(weight_ref.shape[0] // half):
            at = pl.multiple_of(chunk_ref[j] * half, half)
            block = weight_ref[i * half : (i + 1) * half, :]
            total += dot(hidden_ref[0, :, pl.ds(at, half)], block, ((1,), (0,)))
            j += 1
    out_ref[...] = total.astype(out_ref.dtype)


def project(chunks, hidden, weights, start, kind):
    half = sum(weight.shape[0] for weight in weights) // len(chunks)
    return pl.pallas_call(
        functools.partial(project_kernel, half),
        out_shape=jax.ShapeDtypeStruct(start.shape, kind),
        in_specs=[SMEM] + [VMEM] * (2 + len(weights)),
        out_specs=VMEM,
        compiler_params=pltpu.CompilerParams(vmem_limit_bytes=LIMIT),
        name="project",
    )(jnp.stack(chunks).astype(jnp.int32), hidden, start, *weights)


def put_scalars(out_ref, at, tails):
    parts = pieces(jnp.sum(tails, axis=0, keepdims=True))
    out_ref[at:, :] = jnp.zeros((PAD, out_ref.shape[1]), out_ref.dtype)
    for i, part in enumerate(parts):
        out_ref[at + i : at + i + 1, :] = part


def grad_kernel(half, core_ref, near_ref, far_ref, hidden_ref, feats_ref, out_ref):
    chips = out_ref.shape[0]
    slab = half // chips
    step = max(slab, 128)
    near, far = [
        [ref[i * BLOCK : (i + 1) * BLOCK, :] for i in range(2)] for ref in (near_ref, far_ref)
    ]
    for f in range(feats_ref.shape[1] // half):
        for at in range(0, half, step):
            mine = pl.multiple_of((2 * f + core_ref[0]) * half + at, step)
            near_feats = hidden_ref[0, :, pl.ds(mine, step)]
            far_feats = feats_ref[:, f * half + at : f * half + at + step]
            turned = sum(dot(part, near_feats, ((0,), (0,))) for part in near)
            turned += sum(dot(part, far_feats, ((0,), (0,))) for part in far)
            turned = turned.T.astype(out_ref.dtype)
            for i in range(step // slab):
                rows = turned[i * slab : (i + 1) * slab]
                out_ref[at // slab + i, f * slab : (f + 1) * slab, :] = rows
    tails = [ref[2 * BLOCK :, :].astype(jnp.float32) for ref in (near_ref, far_ref)]
    for q in range(chips):
        put_scalars(out_ref.at[q], out_ref.shape[1] - PAD, tails[0] + tails[1])


def weight_grad(core, near, far, hidden, feats, half, chips):
    fsdp = feats.shape[1] // half
    rows = fsdp * half // chips + PAD
    return pl.pallas_call(
        functools.partial(grad_kernel, half),
        out_shape=jax.ShapeDtypeStruct((chips, rows, near.shape[1]), jnp.bfloat16),
        in_specs=[SMEM] + [VMEM] * 4,
        out_specs=VMEM,
        compiler_params=pltpu.CompilerParams(vmem_limit_bytes=LIMIT),
        name="weight_grad",
    )(core.reshape(1), near, far, hidden, feats)


def add_chips_kernel(grad_ref, out_ref):
    fsdp, slab = out_ref.shape[0], out_ref.shape[1] - PAD
    total = jnp.sum(grad_ref[...].astype(jnp.float32), axis=0)
    for f in range(fsdp):
        out_ref[f, :slab, :] = total[f * slab : (f + 1) * slab].astype(out_ref.dtype)
        put_scalars(out_ref.at[f], slab, total[fsdp * slab :])


def add_chips(grad, fsdp):
    _, rows, width = grad.shape
    return pl.pallas_call(
        add_chips_kernel,
        out_shape=jax.ShapeDtypeStruct((fsdp, (rows - PAD) // fsdp + PAD, width), jnp.bfloat16),
        in_specs=[VMEM],
        out_specs=VMEM,
        compiler_params=pltpu.CompilerParams(vmem_limit_bytes=LIMIT),
        name="add_chips",
    )(grad)


def add_kernel(grad_ref, out_ref, alog_ref, skip_ref, loss_ref):
    count, slab = grad_ref.shape[0], out_ref.shape[0]
    heads = alog_ref.shape[1]
    total = jnp.sum(grad_ref[...].astype(jnp.float32), axis=0)
    out_ref[...] = total[:slab].astype(out_ref.dtype)
    total = jnp.sum(total[slab:], axis=0, keepdims=True)
    alog_ref[...] = total[:, :heads]
    skip_ref[...] = total[:, heads : 2 * heads]
    loss_ref[...] = total[:, 2 * heads : 2 * heads + 1]


def add_blocks(grad, heads):
    _, rows, width = grad.shape
    return pl.pallas_call(
        add_kernel,
        out_shape=(
            jax.ShapeDtypeStruct((rows - PAD, width), jnp.bfloat16),
            jax.ShapeDtypeStruct((1, heads), jnp.float32),
            jax.ShapeDtypeStruct((1, heads), jnp.float32),
            jax.ShapeDtypeStruct((1, 1), jnp.float32),
        ),
        in_specs=[VMEM],
        out_specs=(VMEM,) * 4,
        compiler_params=pltpu.CompilerParams(vmem_limit_bytes=LIMIT),
        name="add_blocks",
    )(grad)


def finish_kernel(grad_ref, out_ref):
    count = grad_ref.shape[0]
    for q in range(count // 2):
        for r in range(2):
            out_ref[r * (count // 2) + q] = grad_ref[2 * q + r].astype(jnp.float32)


def finish(grad):
    return pl.pallas_call(
        finish_kernel,
        out_shape=jax.ShapeDtypeStruct(grad.shape, jnp.float32),
        in_specs=[VMEM],
        out_specs=VMEM,
        compiler_params=pltpu.CompilerParams(vmem_limit_bytes=LIMIT),
        name="finish",
    )(grad)


def exchange(blocks, axis):
    return lax.all_to_all(blocks, axis, 0, 0, tiled=True)


def swap(block, axis, shift):
    return lax.ppermute(block, axis, [(i, i ^ shift) for i in range(lax.axis_size(axis))])


def local(hidden, values, targets, dt_raw, proj_weight, a_log, skip):
    fsdp, ctx = lax.axis_size("fsdp"), lax.axis_size("ctx")
    mine = lax.axis_index("ctx")
    core = mine % 2
    rows = hidden.shape[1]
    length = rows * ctx
    heads_all = a_log.shape[0]
    inner = values.shape[2]
    cols = inner // ctx
    heads = cols // HDIM
    half = proj_weight.shape[0] // 2
    slab = proj_weight.shape[0] // ctx
    both = proj_weight.shape[1]
    first = mine * heads
    scale = 1.0 / (inner * math.sqrt(fsdp * length))

    shard = lax.axis_index("fsdp")
    others = [shard ^ shift for shift in range(1, fsdp)]

    vt, part = pack_mixer(core, values, targets, dt_raw, proj_weight, ctx)
    near = [swap(part, "fsdp", shift) for shift in range(1, fsdp)]
    vt = exchange(vt, "ctx")
    a_mine = lax.dynamic_slice_in_dim(a_log, first, heads, 0)
    s_mine = lax.dynamic_slice_in_dim(skip, first, heads, 0)
    rates = jnp.tile(-jnp.exp(a_mine), ctx)[:, None]
    send = pack_hidden(1 - core, hidden, half)
    start = jnp.zeros((rows, both), jnp.float32)
    start = project([2 * shard, 2 * shard + 1], hidden, [proj_weight], start, jnp.float32)
    near[0], send, rates, s_mine, start = lax.optimization_barrier(
        (near[0], send, rates, s_mine, start)
    )
    far = [swap(block, "ctx", 1) for block in near]

    near_at = [2 * other + core for other in others]
    far_at = [2 * other + 1 - core for other in others]
    chunks = [at[i] for i in range(fsdp - 1) for at in (near_at, far_at)]
    blocks = [part[i] for i in range(fsdp - 1) for part in (near, far)]
    projection = project(chunks, hidden, blocks, start, jnp.bfloat16)
    projection, vt = lax.optimization_barrier((projection, vt))
    maps = lax.all_gather(projection, "ctx", axis=0, tiled=True)
    maps, send = lax.optimization_barrier((maps, send))
    feats = swap(send, "ctx", 1)

    proj_part, packed = mixer(maps, vt, rates, s_mine, first, scale, heads_all)

    proj_part = exchange(proj_part.reshape(ctx, rows, both), "ctx").astype(jnp.float32)
    proj_grad = jnp.sum(proj_part, axis=0)
    high = lax.reduce_precision(proj_grad, 8, 7)
    proj_grad = [part.astype(jnp.bfloat16) for part in (high, proj_grad - high)]
    proj_grad = jnp.concatenate(proj_grad + [packed], axis=0)
    proj_far = swap(proj_grad, "ctx", 1)

    grad = weight_grad(core, proj_grad, proj_far, hidden, feats, half, ctx // 2)
    chips = [list(range(r, ctx, 2)) for r in range(2)]
    grad = lax.all_to_all(grad, "ctx", 0, 0, tiled=True, axis_index_groups=chips)
    grad = exchange(add_chips(grad, fsdp), "fsdp")
    grad, grad_a, grad_skip, loss = add_blocks(grad, heads_all)
    grad_w = finish(lax.all_gather(grad, "ctx", axis=0)).reshape(ctx * slab, both)
    return (grad_w, grad_a.reshape(heads_all), grad_skip.reshape(heads_all), loss.reshape(()))


def solution(mesh):
    in_specs = (
        P("fsdp", "ctx", None),
        P("fsdp", "ctx", None),
        P("fsdp", "ctx", None),
        P("fsdp", None, "ctx"),
        P("fsdp", None),
        P(),
        P(),
    )
    out_specs = (P("fsdp", None), P(), P(), P())
    return jax.shard_map(local, mesh=mesh, in_specs=in_specs, out_specs=out_specs, check_vma=False)
```
